128 devices in a mesh: grp: 8 (over x, core), dp: 16 (over z, y).
Axes of the slice: x: 4, y: 4, z: 4, core: 2. Of those that a mesh axis runs over, the one named last changes fastest.
Arguments:
- visual: bfloat16 [16, 1024, 3200], P('dp', 'grp'), may hold values from -6 to 6
- projector: bfloat16 [3200, 8192], P('dp', 'grp'), may hold values from -0.109375 to 0.109375
- key_weight: bfloat16 [8192, 512], replicated, may hold values from -0.0625 to 0.0625
- norm_gain: bfloat16 [8192], replicated, may hold values from 0.099609375 to 1.8984375
- cotangent: bfloat16 [16, 4096, 512], P('dp', 'grp'), may hold values from -0.25 to 0.25
- residual: bfloat16 [51200, 8192], P('dp', 'grp'), may hold values from -0.796875 to 0.796875
- counts: int32 [16, 8, 8], P('dp'), may hold values from 0 to 4, as said below
- offsets: int32 [16, 8, 8], P('dp'), may hold values from 0 to 512, as said below
Outputs:
- weight_grad: float32 [3200, 8192], P('dp', 'grp')
- residual_out: bfloat16 [51200, 8192], P('dp', 'grp')
The draws below stay inside these ranges and needn't reach their ends.
Inputs may be any that keep to these rules, and one draw needn't show every extreme that they name: counts[d, s, b] tiles of 32 rows go from encoder shard s to backbone shard b; each source sends all 4 of its tiles, in order of destination; in every data index one backbone shard receives exactly 8 tiles and none receives more, and some source sends all its tiles to one backbone shard. The counts[d, s, b] * 32 rows that backbone shard b receives from source s start at offsets[d, s, b] of its 512 positions; nonempty blocks lie in order of source, do not intersect and end at or before 512; where counts[d, s, b] is 0, offsets[d, s, b] is 512.
All inputs are finite; a program needn't handle non-finite values.
Results may differ from the reference program's by a relative error of at most 0.015.
Values may be sent and summed in bfloat16 or wider, within the bound.
A program may use at most 128 MiB of HBM per device.

```python
import jax
import jax.numpy as jnp
from jax import lax

ENC_D = 3200
PROJ_D = 8192
KV_W = 512
TROWS = 32
TILES_DEV = 4
ROWS_DEV = 128
SEQ = 512
N_GRP = 8
N_DP = 16


def route_counts(key):

    def one_group(group_key):
        busy_key, order_key, lead_key = jax.random.split(group_key, 3)
        rest_tiles = (N_GRP - 1) * TILES_DEV
        busiest = jax.random.randint(busy_key, (), 0, N_GRP).astype(jnp.int32)
        leader = jax.random.randint(lead_key, (), 0, N_GRP).astype(jnp.int32)
        rest_ids = jnp.arange(rest_tiles, dtype=jnp.int32)
        spare_dest = (rest_ids - TILES_DEV) % (N_GRP - 1)
        spare_dest = spare_dest + (spare_dest >= busiest).astype(jnp.int32)
        rest_target = jnp.where(rest_ids < TILES_DEV, busiest, spare_dest)
        rest_target = rest_target[jax.random.permutation(order_key, rest_tiles)]
        other_source = rest_ids // TILES_DEV
        other_source = other_source + (other_source >= leader).astype(jnp.int32)
        dest_ids = jnp.arange(N_GRP, dtype=jnp.int32)
        pair_table = (other_source[:, None, None] == dest_ids[None, :, None]) & (rest_target[:, None, None] == dest_ids[None, None, :])
        rest_table = jnp.sum(pair_table.astype(jnp.int32), axis=0, dtype=jnp.int32)
        lead_table = ((dest_ids[:, None] == leader) & (dest_ids[None, :] == busiest)).astype(jnp.int32) * TILES_DEV
        return rest_table + lead_table
    return jax.vmap(one_group)(jax.random.split(key, N_DP))


def draw_counts(key, part):
    route_table = route_counts(key)
    return route_table


def draw_offsets(key, part):
    route_table = route_counts(key)
    key = jax.random.fold_in(key, 7)
    gap_rows = jax.random.randint(key, (N_DP, N_GRP, N_GRP), 0, SEQ // (2 * N_GRP) + 1).astype(jnp.int32)
    source_ids = jnp.arange(N_GRP, dtype=jnp.int32)
    gap_rows = jnp.where((source_ids == 0)[None, :, None], 0, gap_rows).astype(jnp.int32)
    block_spans = route_table * TROWS + gap_rows
    starts = jnp.cumsum(block_spans, axis=1, dtype=jnp.int32) - route_table * TROWS
    return jnp.where(route_table > 0, starts, SEQ).astype(jnp.int32)


def levels(stream_key, extent, cuts, least, largest):
    def one(dim, blocks):
        draws = jax.random.uniform(jax.random.fold_in(jax.random.fold_in(stream_key, 6), dim), (blocks,), jnp.float32, least / len(cuts), largest / len(cuts))
        return jnp.repeat(jnp.exp(draws), extent[dim] // blocks).reshape((-1,) + (1,) * (len(extent) - dim - 1))

    level = one(*cuts[0])
    for cut in cuts[1:]:
        level = level * one(*cut)
    return level


def scatter_about(own_key, extent, width, bound, cuts=(), kind=jnp.bfloat16):
    result = width * jax.random.normal(own_key, extent, jnp.float32)
    if cuts:
        result = result * levels(own_key, extent, cuts, -0.22, 0.18)
    return jnp.clip(result, -bound, bound).astype(kind)


def setup_inputs(seed: int = 0) -> dict:
    splits = jax.random.split(jax.random.key(seed), 9)
    return {
        "visual": scatter_about(splits[0], (N_DP, N_GRP * ROWS_DEV, ENC_D), 1.0, 6.0, ((0, 16), (1, 8))),
        "projector": scatter_about(splits[1], (ENC_D, PROJ_D), ENC_D ** -0.5, 0.109375, ((0, 16), (1, 8))),
        "key_weight": scatter_about(splits[2], (PROJ_D, KV_W), PROJ_D ** -0.5, 0.0625),
        "norm_gain": jnp.clip(1.0 + 0.18 * jax.random.normal(splits[3], (PROJ_D,), jnp.float32), 0.099609375, 1.8984375).astype(jnp.bfloat16),
        "cotangent": scatter_about(splits[4], (N_DP, N_GRP * SEQ, KV_W), 0.03125, 0.25, ((0, 16), (1, 8))),
        "residual": scatter_about(splits[5], (N_DP * ENC_D, PROJ_D), 0.1, 0.796875, ((0, 16), (1, 8))),
        "counts": draw_counts(jax.random.fold_in(splits[8], 71), 0),
        "offsets": draw_offsets(jax.random.fold_in(splits[8], 71), 0),
    }


norm_eps = 1e-06
clip_limit = 0.5

def tile_tables(route_table, start_table, tile_count):
    groups = route_table.shape[0]
    dest_ids = jnp.arange(groups, dtype=jnp.int32)
    tile_ids = jnp.arange(tile_count, dtype=jnp.int32)
    through = jnp.cumsum(route_table, axis=1, dtype=jnp.int32)
    before_dest = through - route_table
    before_source = jnp.cumsum(route_table, axis=0, dtype=jnp.int32) - route_table
    target = lax.optimization_barrier(jnp.sum((through[:, None, :] <= tile_ids[None, :, None]).astype(jnp.int32), axis=2, dtype=jnp.int32))
    chosen = (target[:, :, None] == dest_ids[None, None, :]).astype(jnp.int32)
    within = tile_ids[None, :] - lax.optimization_barrier(jnp.sum(chosen * before_dest[:, None, :], axis=2, dtype=jnp.int32))
    slot_tile = lax.optimization_barrier(jnp.sum(chosen * before_source[:, None, :], axis=2, dtype=jnp.int32)) + within
    position = lax.optimization_barrier(jnp.sum(chosen * start_table[:, None, :], axis=2, dtype=jnp.int32)) + within * TROWS
    return (target, slot_tile, position)

def backbone_grad(rows, key_rows, key_weight, norm_gain):
    values = rows.astype(jnp.float32)
    inverse = lax.rsqrt(lax.optimization_barrier(jnp.mean(values * values, axis=-1, keepdims=True)) + norm_eps)
    normed = values * inverse
    upstream = lax.dot_general(key_rows, key_weight, (((1,), (1,)), ((), ())), preferred_element_type=jnp.float32)
    scaled = norm_gain.astype(jnp.float32) * upstream
    inner_mean = lax.optimization_barrier(jnp.mean(normed * scaled, axis=-1, keepdims=True))
    return (inverse * (scaled - normed * inner_mean)).astype(jnp.bfloat16)

def reference(visual, projector, key_weight, norm_gain, cotangent, residual, counts, offsets):
    row_offsets = jnp.arange(TROWS, dtype=jnp.int32)
    summed = jnp.zeros((ENC_D, PROJ_D), jnp.float32)
    pieces = []
    for data_index in range(N_DP):
        target, slot_tile, position = tile_tables(counts[data_index], offsets[data_index], TILES_DEV)
        lookup = ((target * SEQ + position)[:, :, None] + row_offsets).reshape(-1)
        key_rows = jnp.take(cotangent[data_index], lookup, axis=0)
        projected = jnp.dot(visual[data_index], projector, preferred_element_type=jnp.float32).astype(jnp.bfloat16)
        row_grad = backbone_grad(projected, key_rows, key_weight, norm_gain)
        grad_term = lax.dot_general(visual[data_index], row_grad, (((0,), (0,)), ((), ())), preferred_element_type=jnp.float32)
        carried = grad_term + residual[data_index * ENC_D:(data_index + 1) * ENC_D].astype(jnp.float32)
        clipped = jnp.clip(carried, -clip_limit, clip_limit)
        quantized = clipped.astype(jnp.bfloat16)
        pieces.append((carried - clipped).astype(jnp.bfloat16))
        summed = summed + quantized.astype(jnp.float32)
    return (summed, jnp.concatenate(pieces, axis=0))
```

```python
import jax
import jax.numpy as jnp
from jax import lax
from jax.experimental import pallas as pl
from jax.experimental.pallas import tpu as pltpu
from jax.sharding import PartitionSpec as P

MESH = pl.DeviceIdType.MESH
F32 = jnp.float32
BF16 = jnp.bfloat16

norm_eps = 1e-06
clip_limit = 0.5

RING = 4
GROUPS = 8
TROWS = 32
TILES = 4
CAP = 8
ROWS = 128
ALL_ROWS = GROUPS * ROWS
ENC = 3200
BLOCK = 200
PAIR = 2 * BLOCK
WIDTH = 1024
HALF = WIDTH // 2
KEYS = 512
SLOT_ROWS = CAP * TROWS
CHUNKS = 4
CHUNK = WIDTH // CHUNKS


def kernel(
    visual, projector, key_weight, gain, cotangent, residual, counts, offsets,
    grad_out, residual_out,
    v, vt, pj, pf, yv, u, k, kf, kw, cot, onehot, rg, res, qa, qb, ra, rb, ra2, rb2, wg, st,
    local_sem, out_sem,
    v_send, v_recv, k_send, k_recv, p_send, p_recv, s_send, s_recv,
    a_send, a_recv, b_send, b_recv, a2_send, a2_recv, b2_send, b2_recv,
):
    g, d = lax.axis_index("grp"), lax.axis_index("dp")
    x, c = lax.div(g, 2), lax.rem(g, 2)
    z, y = lax.div(d, RING), lax.rem(d, RING)
    s = 1 - 2 * c

    def step(at, n):
        return lax.rem(at + n + 2 * RING, RING)

    def grp_dev(n):
        return (step(x, n) * 2 + c, d)

    other = (x * 2 + 1 - c, d)

    def y_dev(n):
        return (g, z * RING + step(y, n))

    def z_dev(n):
        return (g, step(z, n) * RING + y)

    def remote(src, dst, send, recv, device):
        return pltpu.make_async_remote_copy(
            src, dst, send, recv, device_id=device, device_id_type=MESH
        )

    sent = []

    def start(src, dst, send, recv, device):
        copy = remote(src, dst, send, recv, device)
        copy.start()
        sent.append(copy)

    def arrived(dst, send, recv):
        remote(dst, dst, send, recv, other).wait_recv()

    own_rows = pl.ds(pl.multiple_of(g * ROWS, ROWS), ROWS)
    loads = [
        pltpu.make_async_copy(visual, v.at[own_rows], local_sem.at[0]),
        pltpu.make_async_copy(cotangent, cot, local_sem.at[1]),
        pltpu.make_async_copy(
            key_weight.at[pl.ds(pl.multiple_of(g * WIDTH, WIDTH), WIDTH)], kw, local_sem.at[2]
        ),
        pltpu.make_async_copy(residual, res, local_sem.at[3]),
    ]
    for n in range(CHUNKS):
        loads.append(
            pltpu.make_async_copy(
                projector.at[:, pl.ds(n * CHUNK, CHUNK)], pj.at[n, d], local_sem.at[4 + n]
            )
        )
    for load in loads:
        load.start()

    barrier = pltpu.get_barrier_semaphore()
    friends = [(lax.rem(g + n, GROUPS), d) for n in range(1, GROUPS)]
    friends += [y_dev(1), y_dev(-1), z_dev(1), z_dev(-1)]
    for friend in friends:
        pl.semaphore_signal(barrier, inc=1, device_id=friend, device_id_type=MESH)
    pl.semaphore_wait(barrier, len(friends))

    def x_slot(n, core):
        return step(x, n) * 2 + core

    class Gather:
        def __init__(self, buf, rows, send, recv):
            self.buf, self.rows, self.send, self.recv = buf, rows, send, recv

        def at(self, slot):
            return self.buf.at[pl.ds(pl.multiple_of(slot * self.rows, self.rows), self.rows)]

        def go(self, m, src_slot, device, src=None):
            here = self.at(src_slot)
            start(here if src is None else src, here, self.send.at[m], self.recv.at[m], device)

        def wait(self, m, slot):
            arrived(self.at(slot), self.send.at[m], self.recv.at[m])

        def own(self, src=None):
            self.go(0, g, grp_dev(s), src)
            self.go(1, g, grp_dev(-s), src)
            self.go(3, g, other, src)

        def near(self):
            self.wait(0, x_slot(-s, c))
            self.go(2, x_slot(-s, c), grp_dev(s))
            self.go(4, x_slot(-s, c), other)
            self.wait(1, x_slot(s, c))
            self.go(5, x_slot(s, c), other)

        def far(self):
            self.wait(2, x_slot(2, c))
            self.go(6, x_slot(2, c), other)

        def near_other(self):
            self.wait(3, x_slot(0, 1 - c))
            self.wait(4, x_slot(s, 1 - c))
            self.wait(5, x_slot(-s, 1 - c))

        def far_other(self):
            self.wait(6, x_slot(2, 1 - c))

    rows = Gather(v, ROWS, v_send, v_recv)
    keys = Gather(k, CAP, k_send, k_recv)

    rows.own(visual)

    def p_slot(n, first, second):
        if n % 2 == 0:
            return step(z, second) * RING + step(y, first)
        return step(z, first) * RING + step(y, second)

    def p_go(n, m, slot, device, src=None):
        here = pj.at[n, slot]
        start(here if src is None else src, here, p_send.at[n, m], p_recv.at[n, m], device)

    def p_wait(n, m, slot):
        arrived(pj.at[n, slot], p_send.at[n, m], p_recv.at[n, m])

    def first_dev(n, by):
        return y_dev(by) if n % 2 == 0 else z_dev(by)

    def second_dev(n, by):
        return z_dev(by) if n % 2 == 0 else y_dev(by)

    firsts = (0, -s, s, 2)

    def p_spread(n, j, src=None):
        slot = p_slot(n, firsts[j], 0)
        p_go(n, 3 + 3 * j, slot, second_dev(n, s), src)
        p_go(n, 4 + 3 * j, slot, second_dev(n, -s), src)

    def p_own(n):
        src = pj.at[n, d]
        p_go(n, 0, d, first_dev(n, s), src)
        p_go(n, 1, d, first_dev(n, -s), src)

    def p_first(n):
        p_wait(n, 0, p_slot(n, -s, 0))
        p_go(n, 2, p_slot(n, -s, 0), first_dev(n, s))

    def p_first_spread(n):
        p_spread(n, 1)
        p_wait(n, 1, p_slot(n, s, 0))
        p_spread(n, 2)
        p_wait(n, 2, p_slot(n, 2, 0))
        p_spread(n, 3)

    def p_second(n, j):
        p_wait(n, 3 + 3 * j, p_slot(n, firsts[j], -s))
        p_go(n, 5 + 3 * j, p_slot(n, firsts[j], -s), second_dev(n, s))

    def p_last(n):
        for j in range(RING):
            p_wait(n, 4 + 3 * j, p_slot(n, firsts[j], s))
            p_wait(n, 5 + 3 * j, p_slot(n, firsts[j], 2))

    for n in range(CHUNKS):
        loads[4 + n].wait()
        p_own(n)
    for n in range(CHUNKS):
        p_spread(n, 0)

    tiles = []
    earlier = [jnp.int32(0)] * GROUPS
    for source in range(GROUPS):
        route = [counts[source, b] for b in range(GROUPS)]
        first = [offsets[source, b] for b in range(GROUPS)]
        for t in range(TILES):
            target, slot, position = jnp.int32(0), jnp.int32(0), jnp.int32(0)
            passed = jnp.int32(0)
            for b in range(GROUPS):
                hit = (passed <= t) & (t < passed + route[b])
                within = t - passed
                target = jnp.where(hit, b, target)
                slot = jnp.where(hit, earlier[b] + within, slot)
                position = jnp.where(hit, first[b] + within * TROWS, position)
                passed = passed + route[b]
            slot = jnp.clip(slot, 0, CAP - 1)
            tiles.append((target, slot, position))
        earlier = [e + r for e, r in zip(earlier, route)]
    slot_iota = (
        lax.broadcasted_iota(jnp.int32, (TROWS, KEYS), 1)
        - lax.broadcasted_iota(jnp.int32, (TROWS, KEYS), 0)
    )
    for i in range(CAP):
        place = jnp.int32(-4096)
        for target, slot, position in tiles:
            place = jnp.where((target == g) & (slot == i), position, place)
        onehot[i * TROWS : (i + 1) * TROWS, :] = jnp.where(slot_iota == place, 1.0, 0.0).astype(BF16)
    loads[1].wait()
    k[pl.ds(g * CAP, CAP)] = jnp.dot(
        onehot[...], cot[...], preferred_element_type=F32
    ).astype(BF16).reshape(CAP, TROWS, KEYS)
    keys.own()

    def transpose(slot):
        @pl.loop(0, 5)
        def _(i):
            cols = pl.ds(pl.multiple_of(i * 640, 640), 640)
            block = v[pl.ds(pl.multiple_of(slot * ROWS, ROWS), ROWS), cols]
            vt[cols, pl.ds(pl.multiple_of(slot * ROWS, ROWS), ROWS)] = block.T

    def project(n):
        @pl.loop(0, 8)
        def _(i):
            low = pj[n, 2 * i].astype(F32)
            high = pj[n, 2 * i + 1].astype(F32)
            pf[pl.ds(pl.multiple_of(i * PAIR, PAIR), PAIR), :] = jnp.concatenate(
                [low, high], axis=0
            ).astype(BF16)

        @pl.loop(0, 2)
        def _(i):
            part = pl.ds(pl.multiple_of(i * 512, 512), 512)
            yv[part, n * CHUNK : (n + 1) * CHUNK] = jnp.dot(
                v[part, :], pf[...], preferred_element_type=F32
            ).astype(BF16)

    loads[0].wait()
    loads[2].wait()
    for n in range(CHUNKS):
        p_first(n)
    for n in range(CHUNKS):
        p_first_spread(n)
    transpose(g)
    for n in (0, 1):
        for j in range(RING):
            p_second(n, j)
    rows.near()
    for n in (2, 3):
        for j in (0, 1):
            p_second(n, j)
    keys.near()
    transpose(x_slot(-s, c))
    for n in (2, 3):
        for j in (2, 3):
            p_second(n, j)
    rows.far()
    transpose(x_slot(s, c))
    rows.near_other()
    transpose(x_slot(0, 1 - c))
    transpose(x_slot(-s, 1 - c))
    transpose(x_slot(s, 1 - c))
    transpose(x_slot(2, c))
    keys.far()
    rows.far_other()
    transpose(x_slot(2, 1 - c))
    for n in (0, 1):
        p_last(n)
        project(n)
    keys.near_other()
    keys.far_other()
    for i, (target, slot, _) in enumerate(tiles):
        kf[i * TROWS : (i + 1) * TROWS, :] = k[target * CAP + slot]
    gains = gain[pl.ds(g, 1), :]

    @pl.loop(0, 2)
    def _(i):
        part = pl.ds(pl.multiple_of(i * 512, 512), 512)
        u[part, :] = gains * lax.dot_general(
            kf[part, :], kw[...], (((1,), (1,)), ((), ())), preferred_element_type=F32
        )

    for n in (2, 3):
        p_last(n)
        project(n)

    for i in range(GROUPS):
        part = slice(i * ROWS, (i + 1) * ROWS)
        squares = jnp.zeros((ROWS, 128), F32)
        products = jnp.zeros((ROWS, 128), F32)
        for j in range(WIDTH // 128):
            cols = slice(j * 128, (j + 1) * 128)
            value = yv[part, cols].astype(F32)
            squares += value * value
            products += value * u[part, cols]
        st[g, pl.ds(i, 1), :] = jnp.sum(squares.T, axis=0, keepdims=True)
        st[g, pl.ds(GROUPS + i, 1), :] = jnp.sum(products.T, axis=0, keepdims=True)
    for n in range(1, GROUPS):
        start(st.at[g], st.at[g], s_send.at[n], s_recv.at[n], (lax.rem(g + n, GROUPS), d))
    for n in range(1, GROUPS):
        arrived(st.at[lax.rem(g - n + GROUPS, GROUPS)], s_send.at[n], s_recv.at[n])
    total = st[0]
    for n in range(1, GROUPS):
        total = total + st[n]
    mean = total * (1.0 / (GROUPS * WIDTH))
    inverse = lax.rsqrt(mean[:GROUPS] + norm_eps)
    inner = inverse * mean[GROUPS:]
    for i in range(GROUPS):
        part = slice(i * ROWS, (i + 1) * ROWS)
        inv = jnp.broadcast_to(inverse[i : i + 1], (ROWS, 128)).T
        inn = jnp.broadcast_to((inverse * inner)[i : i + 1], (ROWS, 128)).T
        for j in range(WIDTH // 128):
            cols = slice(j * 128, (j + 1) * 128)
            value = yv[part, cols].astype(F32)
            rg[part, cols] = (inv * (u[part, cols] - value * inn)).astype(BF16)

    loads[3].wait()
    lead_y = 1 - lax.div(y, 2)
    lead_z = 1 - lax.div(z, 2)

    def ordered(lead, i):
        return lax.rem(lead + i, 2)

    def unit(p, half):
        part = pl.ds(pl.multiple_of(p * PAIR, PAIR), PAIR)
        cols = slice(half * HALF, (half + 1) * HALF)
        term = jnp.dot(vt[part, :], rg[:, cols], preferred_element_type=F32)
        carried = term + res[part, cols].astype(F32)
        clipped = jnp.clip(carried, -clip_limit, clip_limit)
        res[part, cols] = (carried - clipped).astype(BF16)
        return clipped[:BLOCK].astype(BF16), clipped[BLOCK:].astype(BF16)

    def a_copy(m, i, by, device):
        return remote(
            qa.at[step(z, by) * 2 + ordered(lead_y, i)], ra.at[2 * m + i],
            a_send.at[m, i], a_recv.at[m, i], device,
        )

    def b_copy(m, i, by, device):
        return remote(
            qb.at[step(y, by) * 2 + ordered(lead_z, i)], rb.at[2 * m + i],
            b_send.at[m, i], b_recv.at[m, i], device,
        )

    @pl.loop(0, 8)
    def _(i):
        turn, which = lax.div(i, 2), lax.rem(i, 2)
        by = jnp.where(turn == 0, 2, jnp.where(turn == 1, -s, jnp.where(turn == 2, s, 0)))
        p = step(z, by) * 2 + ordered(lead_y, which)
        low, high = unit(p, 0)
        qa[p, 0] = low
        qa[p, 1] = high

        @pl.when(turn == 0)
        def _():
            a_copy(0, which, 2, z_dev(s)).start()

        @pl.when(turn == 1)
        def _():
            a_copy(1, which, -s, z_dev(-s)).start()

        pair = ordered(lead_y, lax.div(i, 4))
        plane = lax.rem(2 * lead_z + lax.rem(i, 4), RING)
        low, high = unit(plane * 2 + pair, 1)
        at = lax.div(plane, 2)
        qb[4 * pair + at, lax.rem(plane, 2)] = low
        qb[4 * pair + 2 + at, lax.rem(plane, 2)] = high

        @pl.when(i == 1)
        def _():
            b_copy(0, 0, 2, y_dev(s)).start()

        @pl.when(i == 3)
        def _():
            b_copy(0, 1, 2, y_dev(s)).start()

        @pl.when(i == 5)
        def _():
            b_copy(1, 0, -s, y_dev(-s)).start()

        @pl.when(i == 7)
        def _():
            b_copy(1, 1, -s, y_dev(-s)).start()

    store = pltpu.make_async_copy(res, residual_out, out_sem.at[0])
    store.start()

    def add(buf, index, terms):
        for j in range(2):
            value = buf[index, j].astype(F32)
            for term_buf, term_index in terms:
                value = value + term_buf[term_index, j].astype(F32)
            buf[index, j] = value.astype(BF16)

    for i in range(2):
        a_copy(0, i, 2, z_dev(s)).wait_recv()
        add(qa, step(z, s) * 2 + ordered(lead_y, i), [(ra, i)])
        a_copy(2, i, s, z_dev(s)).start()
        b_copy(0, i, 2, y_dev(s)).wait_recv()
        add(qb, step(y, s) * 2 + ordered(lead_z, i), [(rb, i)])
        b_copy(2, i, s, y_dev(s)).start()

    def a_block(by):
        yy = step(y, by)
        return (2 * z + lax.div(yy, 2), lax.rem(yy, 2))

    def b_block(by):
        zz = step(z, by)
        return (2 * y + lax.div(zz, 2), lax.rem(zz, 2))

    def a2_copy(m, by, device):
        return remote(qa.at[a_block(by)], ra2.at[m], a2_send.at[m], a2_recv.at[m], device)

    def b2_copy(m, by, device):
        return remote(qb.at[b_block(by)], rb2.at[m], b2_send.at[m], b2_recv.at[m], device)

    for i in range(2):
        for m in (1, 2):
            a_copy(m, i, 0, other).wait_recv()
            b_copy(m, i, 0, other).wait_recv()
        add(qa, 2 * z + ordered(lead_y, i), [(ra, 2 + i), (ra, 4 + i)])
        add(qb, 2 * y + ordered(lead_z, i), [(rb, 2 + i), (rb, 4 + i)])
        if i == 0:
            a2_copy(0, 2, y_dev(s)).start()
            b2_copy(0, 2, z_dev(s)).start()
    a2_copy(1, -s, y_dev(-s)).start()
    b2_copy(1, -s, z_dev(-s)).start()
    a2_copy(0, 2, y_dev(s)).wait_recv()
    qa[a_block(s)] = (qa[a_block(s)].astype(F32) + ra2[0].astype(F32)).astype(BF16)
    a2_copy(2, s, y_dev(s)).start()
    b2_copy(0, 2, z_dev(s)).wait_recv()
    qb[b_block(s)] = (qb[b_block(s)].astype(F32) + rb2[0].astype(F32)).astype(BF16)
    b2_copy(2, s, z_dev(s)).start()
    a2_copy(1, 0, other).wait_recv()
    a2_copy(2, 0, other).wait_recv()
    wg[:, :HALF] = qa[a_block(0)].astype(F32) + ra2[1].astype(F32) + ra2[2].astype(F32)
    b2_copy(1, 0, other).wait_recv()
    b2_copy(2, 0, other).wait_recv()
    wg[:, HALF:] = qb[b_block(0)].astype(F32) + rb2[1].astype(F32) + rb2[2].astype(F32)
    last = pltpu.make_async_copy(wg, grad_out, out_sem.at[1])
    last.start()

    for copy in sent:
        copy.wait_send()
    for i in range(2):
        for m, by in enumerate((2, -s, s)):
            a_copy(m, i, by, other).wait_send()
            b_copy(m, i, by, other).wait_send()
    for m, by in enumerate((2, -s, s)):
        a2_copy(m, by, other).wait_send()
        b2_copy(m, by, other).wait_send()
    store.wait()
    last.wait()


def per_device(visual, projector, key_weight, norm_gain, cotangent, residual, counts, offsets):
    gain = norm_gain.astype(F32).reshape(GROUPS, WIDTH)
    anywhere = pl.BlockSpec(memory_space=pl.ANY)
    scalars = pl.BlockSpec(memory_space=pltpu.SMEM)
    dma = pltpu.SemaphoreType.DMA
    return pl.pallas_call(
        kernel,
        out_shape=(
            jax.ShapeDtypeStruct((BLOCK, WIDTH), F32),
            jax.ShapeDtypeStruct((ENC, WIDTH), BF16),
        ),
        in_specs=[
            anywhere, anywhere, anywhere, pl.BlockSpec(memory_space=pltpu.VMEM), anywhere, anywhere,
            scalars, scalars,
        ],
        out_specs=(anywhere, anywhere),
        scratch_shapes=[
            pltpu.VMEM((ALL_ROWS, ENC), BF16),
            pltpu.VMEM((ENC, ALL_ROWS), BF16),
            pltpu.VMEM((CHUNKS, 16, BLOCK, CHUNK), BF16),
            pltpu.VMEM((ENC, CHUNK), BF16),
            pltpu.VMEM((ALL_ROWS, WIDTH), BF16),
            pltpu.VMEM((ALL_ROWS, WIDTH), F32),
            pltpu.VMEM((GROUPS * CAP, TROWS, KEYS), BF16),
            pltpu.VMEM((ALL_ROWS, KEYS), BF16),
            pltpu.VMEM((WIDTH, KEYS), BF16),
            pltpu.VMEM((512, KEYS), BF16),
            pltpu.VMEM((SLOT_ROWS, 512), BF16),
            pltpu.VMEM((ALL_ROWS, WIDTH), BF16),
            pltpu.VMEM((ENC, WIDTH), BF16),
            pltpu.VMEM((8, 2, BLOCK, HALF), BF16),
            pltpu.VMEM((8, 2, BLOCK, HALF), BF16),
            pltpu.VMEM((6, 2, BLOCK, HALF), BF16),
            pltpu.VMEM((6, 2, BLOCK, HALF), BF16),
            pltpu.VMEM((3, BLOCK, HALF), BF16),
            pltpu.VMEM((3, BLOCK, HALF), BF16),
            pltpu.VMEM((BLOCK, WIDTH), F32),
            pltpu.VMEM((GROUPS, 2 * GROUPS, 128), F32),
            dma((8,)), dma((2,)),
            dma((7,)), dma((7,)), dma((7,)), dma((7,)),
            dma((CHUNKS, 15)), dma((CHUNKS, 15)), dma((GROUPS,)), dma((GROUPS,)),
            dma((3, 2)), dma((3, 2)), dma((3, 2)), dma((3, 2)),
            dma((3,)), dma((3,)), dma((3,)), dma((3,)),
        ],
        compiler_params=pltpu.CompilerParams(
            collective_id=0, has_side_effects=True, vmem_limit_bytes=62 * 2**20
        ),
        cost_estimate=pl.CostEstimate(flops=16 * 10**9, bytes_accessed=20 * 10**6, transcendentals=0),
    )(
        visual[0], projector, key_weight, gain, cotangent[0], residual, counts[0], offsets[0]
    )


def solution(mesh):
    placed = (
        P("dp", "grp", None),
        P("dp", "grp"),
        P(),
        P(),
        P("dp", "grp", None),
        P("dp", "grp"),
        P("dp", None, None),
        P("dp", None, None),
    )
    return jax.shard_map(
        per_device,
        mesh=mesh,
        in_specs=placed,
        out_specs=(P("dp", "grp"), P("dp", "grp")),
        check_vma=False,
    )
```

```python
import jax
import jax.numpy as jnp
from jax import lax
from jax.experimental import pallas as pl
from jax.experimental.pallas import tpu as pltpu
from jax.sharding import PartitionSpec as P

MESH = pl.DeviceIdType.MESH
F32 = jnp.float32
BF16 = jnp.bfloat16

norm_eps = 1e-06
clip_limit = 0.5

RING = 4
GROUPS = 8
TROWS = 32
TILES = 4
CAP = 8
ROWS = 128
ALL_ROWS = GROUPS * ROWS
ENC = 3200
BLOCK = 200
PAIR = 2 * BLOCK
WIDTH = 1024
HALF = WIDTH // 2
PARTS = ((0, 256), (256, 256))
KEYS = 512
SLOT_ROWS = CAP * TROWS
CHUNKS = 4
WIDE, NARROW = 384, 128
ROW_PIECES, KEY_PIECES = 4, 2


def kernel(
    visual, projector, key_weight, gain, cotangent, residual, counts, offsets,
    wg, res,
    v, vt, wide, narrow, pf, yv, u, k, kf, kw, cot, onehot, rg, gains, st,
    qa0, qa1, qb0, qb1, ra0, ra1, rb0, rb1, ra20, ra21, rb20, rb21,
    local_sem,
    v_send, v_recv, v_other, k_send, k_recv, k_other, p_send, p_recv, p_end, s_send, s_recv,
    q_send, q_long, q_near, q2_send, q2_long, q2_near,
):
    g, d = lax.axis_index("grp"), lax.axis_index("dp")
    x, c = lax.div(g, 2), lax.rem(g, 2)
    z, y = lax.div(d, RING), lax.rem(d, RING)
    s = 1 - 2 * c

    def step(at, n):
        return lax.rem(at + n + 2 * RING, RING)

    def grp_dev(n):
        return (step(x, n) * 2 + c, d)

    other = (x * 2 + 1 - c, d)

    def y_dev(n):
        return (g, z * RING + step(y, n))

    def z_dev(n):
        return (g, step(z, n) * RING + y)

    def remote(src, dst, send, recv, device):
        return pltpu.make_async_remote_copy(
            src, dst, send, recv, device_id=device, device_id_type=MESH
        )

    def start(src, dst, send, recv, device):
        remote(src, dst, send, recv, device).start()

    def done(like, sem):
        pltpu.make_async_copy(like, like, sem).wait()

    own_rows = pl.ds(pl.multiple_of(g * ROWS, ROWS), ROWS)
    loads = [
        pltpu.make_async_copy(visual, v.at[own_rows], local_sem.at[0]),
        pltpu.make_async_copy(cotangent, cot, local_sem.at[1]),
        pltpu.make_async_copy(
            key_weight.at[pl.ds(pl.multiple_of(g * WIDTH, WIDTH), WIDTH)], kw, local_sem.at[2]
        ),
        pltpu.make_async_copy(residual, res, local_sem.at[3]),
    ]

    def chunk_cols(n):
        return (n * WIDE, WIDE) if n < 2 else (2 * WIDE + (n - 2) * NARROW, NARROW)

    def pj(n, slot):
        return wide.at[n, slot] if n < 2 else narrow.at[n - 2, slot]

    for n in range(CHUNKS):
        loads.append(
            pltpu.make_async_copy(
                projector.at[:, pl.ds(*chunk_cols(n))], pj(n, d), local_sem.at[4 + n]
            )
        )
    loads.append(
        pltpu.make_async_copy(
            gain.at[pl.ds(pl.multiple_of(g * WIDTH, WIDTH), WIDTH)], gains, local_sem.at[8]
        )
    )
    for load in loads:
        load.start()

    barrier = pltpu.get_barrier_semaphore()
    friends = [(lax.rem(g + n, GROUPS), d) for n in range(1, GROUPS)]
    friends += [y_dev(1), y_dev(-1), z_dev(1), z_dev(-1)]
    for friend in friends:
        pl.semaphore_signal(barrier, inc=1, device_id=friend, device_id_type=MESH)
    pl.semaphore_wait(barrier, len(friends))

    def x_slot(n, core):
        return step(x, n) * 2 + core

    class Gather:
        def __init__(self, buf, rows, pieces, send, recv, other_recv):
            self.buf, self.rows, self.send, self.recv = buf, rows, send, recv
            self.other = other_recv
            self.pieces, self.piece = pieces, rows // pieces

        def at(self, slot, i):
            row = pl.multiple_of(slot * self.rows + i * self.piece, self.piece)
            return self.buf.at[pl.ds(row, self.piece)]

        def go(self, m, i, slot, device):
            here = self.at(slot, i)
            start(here, here, self.send, self.recv.at[m, i], device)

        def give(self, m, i, slot):
            here = self.at(slot, i)
            start(here, here, self.send, self.other.at[m], other)

        def own(self, i):
            self.go(0, i, g, grp_dev(s))
            self.go(1, i, g, grp_dev(-s))

        def own_other(self, i):
            self.give(0, i, g)

        def near(self, i):
            done(self.at(x_slot(-s, c), i), self.recv.at[0, i])
            self.go(2, i, x_slot(-s, c), grp_dev(s))
            self.give(1, i, x_slot(-s, c))
            done(self.at(x_slot(s, c), i), self.recv.at[1, i])
            self.give(2, i, x_slot(s, c))

        def far(self, i):
            done(self.at(x_slot(2, c), i), self.recv.at[2, i])
            self.give(3, i, x_slot(2, c))

        def from_other(self, m):
            done(self.buf.at[pl.ds(0, self.rows)], self.other.at[m])

    rows = Gather(v, ROWS, ROW_PIECES, v_send.at[0], v_recv, v_other)
    keys = Gather(k, CAP, KEY_PIECES, k_send.at[0], k_recv, k_other)

    loads[0].wait()
    for i in range(ROW_PIECES):
        rows.own(i)

    def p_slot(n, first, second):
        if n % 2 == 0:
            return step(z, second) * RING + step(y, first)
        return step(z, first) * RING + step(y, second)

    def p_go(n, recv, slot, device):
        start(pj(n, slot), pj(n, slot), p_send.at[n], recv, device)

    def p_wait(n, m, slot):
        done(pj(n, slot), p_recv.at[n, m])

    def first_dev(n, by):
        return y_dev(by) if n % 2 == 0 else z_dev(by)

    def second_dev(n, by):
        return z_dev(by) if n % 2 == 0 else y_dev(by)

    firsts = (0, -s, s, 2)

    def p_spread(n, j):
        slot = p_slot(n, firsts[j], 0)
        p_go(n, p_recv.at[n, 3 + j], slot, second_dev(n, s))
        p_go(n, p_end.at[n], slot, second_dev(n, -s))

    def p_own(n):
        p_go(n, p_recv.at[n, 0], d, first_dev(n, s))
        p_go(n, p_recv.at[n, 1], d, first_dev(n, -s))

    def p_first(n):
        p_wait(n, 0, p_slot(n, -s, 0))
        p_go(n, p_recv.at[n, 2], p_slot(n, -s, 0), first_dev(n, s))

    def p_first_spread(n):
        p_spread(n, 1)
        p_wait(n, 1, p_slot(n, s, 0))
        p_spread(n, 2)
        p_wait(n, 2, p_slot(n, 2, 0))
        p_spread(n, 3)

    def p_second(n, j):
        p_wait(n, 3 + j, p_slot(n, firsts[j], -s))
        p_go(n, p_end.at[n], p_slot(n, firsts[j], -s), second_dev(n, s))

    def p_slots(n, count):
        return wide.at[n, pl.ds(0, count)] if n < 2 else narrow.at[n - 2, pl.ds(0, count)]

    def p_last(n):
        done(p_slots(n, 8), p_end.at[n])

    for n in range(CHUNKS):
        loads[4 + n].wait()
        p_own(n)

    tiles = []
    earlier = [jnp.int32(0)] * GROUPS
    for source in range(GROUPS):
        route = [counts[source, b] for b in range(GROUPS)]
        first = [offsets[source, b] for b in range(GROUPS)]
        for t in range(TILES):
            target, slot, position = jnp.int32(0), jnp.int32(0), jnp.int32(0)
            passed = jnp.int32(0)
            for b in range(GROUPS):
                hit = (passed <= t) & (t < passed + route[b])
                within = t - passed
                target = jnp.where(hit, b, target)
                slot = jnp.where(hit, earlier[b] + within, slot)
                position = jnp.where(hit, first[b] + within * TROWS, position)
                passed = passed + route[b]
            slot = jnp.clip(slot, 0, CAP - 1)
            tiles.append((target, slot, position))
        earlier = [e + r for e, r in zip(earlier, route)]
    slot_iota = (
        lax.broadcasted_iota(jnp.int32, (TROWS, KEYS), 1)
        - lax.broadcasted_iota(jnp.int32, (TROWS, KEYS), 0)
    )
    for i in range(CAP):
        place = jnp.int32(-4096)
        for target, slot, position in tiles:
            place = jnp.where((target == g) & (slot == i), position, place)
        onehot[i * TROWS : (i + 1) * TROWS, :] = jnp.where(slot_iota == place, 1.0, 0.0).astype(BF16)
    loads[1].wait()
    k[pl.ds(g * CAP, CAP)] = jnp.dot(
        onehot[...], cot[...], preferred_element_type=F32
    ).astype(BF16).reshape(CAP, TROWS, KEYS)
    def transpose(slot):
        @pl.loop(0, 5)
        def _(i):
            cols = pl.ds(pl.multiple_of(i * 640, 640), 640)
            block = v[pl.ds(pl.multiple_of(slot * ROWS, ROWS), ROWS), cols]
            vt[cols, pl.ds(pl.multiple_of(slot * ROWS, ROWS), ROWS)] = block.T

    def assemble(pair):
        bufs, width = ((wide, WIDE), (narrow, NARROW))[pair]

        @pl.loop(0, 8)
        def _(i):
            part = pl.ds(pl.multiple_of(i * PAIR, PAIR), PAIR)
            for n in range(2):
                both = [bufs[n, 2 * i].astype(F32), bufs[n, 2 * i + 1].astype(F32)]
                pf[part, n * width : (n + 1) * width] = jnp.concatenate(both, axis=0).astype(BF16)

    def project(pair, i):
        first, last = ((0, 2 * WIDE), (2 * WIDE, WIDTH))[pair]
        part = slice(i * 512, (i + 1) * 512)
        yv[part, first:last] = jnp.dot(
            v[part, :], pf[:, : last - first], preferred_element_type=F32
        ).astype(BF16)

    for n in (0, 1):
        p_first(n)
    for n in (0, 1):
        p_spread(n, 0)
    for i in range(ROW_PIECES):
        rows.own_other(i)
    for n in (2, 3):
        p_first(n)
    for n in (0, 1):
        p_first_spread(n)
    for n in (2, 3):
        p_spread(n, 0)
    rows.near(0)
    for n in (2, 3):
        p_first_spread(n)
    transpose(g)
    for n in (0, 1):
        p_second(n, 0)
    rows.near(1)
    rows.from_other(0)
    transpose(x_slot(0, 1 - c))
    rows.near(2)
    for i in range(KEY_PIECES):
        keys.own(i)
        keys.own_other(i)
    for n in (0, 1):
        p_second(n, 1)
    rows.near(3)
    for n in (0, 1):
        p_second(n, 2)
    transpose(x_slot(-s, c))
    rows.far(0)
    transpose(x_slot(s, c))
    rows.far(1)
    for n in (0, 1):
        p_second(n, 3)
    rows.from_other(1)
    transpose(x_slot(s, 1 - c))
    rows.far(2)
    rows.from_other(2)
    transpose(x_slot(-s, 1 - c))
    rows.far(3)
    for n in (2, 3):
        for j in (0, 1):
            p_second(n, j)
    transpose(x_slot(2, c))
    for n in (0, 1):
        p_last(n)
    assemble(0)
    for n in (2, 3):
        for j in (2, 3):
            p_second(n, j)
    keys.near(0)
    rows.from_other(3)
    project(0, 0)
    keys.near(1)
    project(0, 1)
    keys.far(0)
    for n in (2, 3):
        p_last(n)
    assemble(1)
    project(1, 0)
    keys.far(1)
    project(1, 1)
    for m in range(4):
        keys.from_other(m)
    for i, (target, slot, _) in enumerate(tiles):
        kf[i * TROWS : (i + 1) * TROWS, :] = k[target * CAP + slot]
    loads[2].wait()
    loads[8].wait()
    gain_row = gains[...].astype(F32).reshape(1, WIDTH)
    for i in range(2):
        part = slice(i * 512, (i + 1) * 512)
        u[part, :] = gain_row * lax.dot_general(
            kf[part, :], kw[...], (((1,), (1,)), ((), ())), preferred_element_type=F32
        )

    for i in range(GROUPS):
        part = slice(i * ROWS, (i + 1) * ROWS)
        squares = jnp.zeros((ROWS, 128), F32)
        products = jnp.zeros((ROWS, 128), F32)
        for j in range(WIDTH // 128):
            cols = slice(j * 128, (j + 1) * 128)
            value = yv[part, cols].astype(F32)
            squares += value * value
            products += value * u[part, cols]
        st[g, pl.ds(i, 1), :] = jnp.sum(squares.T, axis=0, keepdims=True)
        st[g, pl.ds(GROUPS + i, 1), :] = jnp.sum(products.T, axis=0, keepdims=True)
    for n in range(1, GROUPS):
        start(st.at[g], st.at[g], s_send.at[0], s_recv.at[0], (lax.rem(g + n, GROUPS), d))
    transpose(x_slot(2, 1 - c))
    done(st.at[pl.ds(0, GROUPS - 1)], s_recv.at[0])
    total = st[0]
    for n in range(1, GROUPS):
        total = total + st[n]
    mean = total * (1.0 / (GROUPS * WIDTH))
    inverse = lax.rsqrt(mean[:GROUPS] + norm_eps)
    inner = inverse * mean[GROUPS:]
    for i in range(GROUPS):
        part = slice(i * ROWS, (i + 1) * ROWS)
        inv = jnp.broadcast_to(inverse[i : i + 1], (ROWS, 128)).T
        inn = jnp.broadcast_to((inverse * inner)[i : i + 1], (ROWS, 128)).T
        for j in range(WIDTH // 128):
            cols = slice(j * 128, (j + 1) * 128)
            value = yv[part, cols].astype(F32)
            rg[part, cols] = (inv * (u[part, cols] - value * inn)).astype(BF16)

    loads[3].wait()
    lead_y = 1 - lax.div(y, 2)
    lead_z = 1 - lax.div(z, 2)

    def unit(p, first, width):
        part = pl.ds(pl.multiple_of(p * PAIR, PAIR), PAIR)
        cols = slice(first, first + width)
        term = jnp.dot(vt[part, :], rg[:, cols], preferred_element_type=F32)
        carried = term + res[part, cols].astype(F32)
        clipped = jnp.clip(carried, -clip_limit, clip_limit)
        res[part, cols] = (carried - clipped).astype(BF16)
        return clipped[:BLOCK].astype(BF16), clipped[BLOCK:].astype(BF16)

    class Sum:
        def __init__(self, n, q, r, r2, at, near, lead, at2, near2):
            self.n, self.q, self.r, self.r2 = n, q, r, r2
            self.at, self.near, self.lead, self.at2, self.near2 = at, near, lead, at2, near2

        def piece(self, by, i):
            return 2 * step(self.at, by) + lax.rem(self.lead + i, 2)

        def send(self, m, i, by, to):
            recv = q_long.at[self.n, i] if m == 0 else q_near.at[self.n, i]
            start(
                self.q.at[self.piece(by, i)], self.r.at[2 * i + m - 1 if m else 4 + i],
                q_send.at[self.n], recv, self.near(to),
            )

        def long(self, i):
            self.send(0, i, 2, s)

        def plain(self, i):
            self.send(1, i, -s, -s)

        def middle(self, i):
            done(self.r.at[4 + i], q_long.at[self.n, i])
            self.add(self.piece(s, i), (4 + i,))
            self.send(2, i, s, s)

        def own(self, i):
            done(self.r.at[pl.ds(2 * i, 2)], q_near.at[self.n, i])
            self.add(self.piece(0, i), (2 * i, 2 * i + 1))

        def add(self, index, terms):
            for j in range(2):
                value = self.q[index, j].astype(F32)
                for term in terms:
                    value = value + self.r[term, j].astype(F32)
                self.q[index, j] = value.astype(BF16)

        def block(self, by):
            at2 = step(self.at2, by)
            return (2 * self.at + lax.div(at2, 2), lax.rem(at2, 2))

        def send2(self, m, by, to):
            recv = q2_long.at[self.n] if m == 0 else q2_near.at[self.n]
            start(
                self.q.at[self.block(by)], self.r2.at[(2, 0, 1)[m]],
                q2_send.at[self.n], recv, self.near2(to),
            )

        def long2(self):
            self.send2(0, 2, s)

        def plain2(self):
            self.send2(1, -s, -s)

        def middle2(self):
            done(self.r2.at[2], q2_long.at[self.n])
            here = self.block(s)
            self.q[here] = (self.q[here].astype(F32) + self.r2[2].astype(F32)).astype(BF16)
            self.send2(2, s, s)

        def finish(self, cols):
            done(self.r2.at[pl.ds(0, 2)], q2_near.at[self.n])
            total = self.q[self.block(0)].astype(F32) + self.r2[0].astype(F32)
            wg[:, cols] = total + self.r2[1].astype(F32)

        def sent(self):
            done(self.r, q_send.at[self.n])
            done(self.r2, q2_send.at[self.n])

    sums = []
    for n, (q_a, r_a, r2_a, q_b, r_b, r2_b) in enumerate(
        ((qa0, ra0, ra20, qb0, rb0, rb20), (qa1, ra1, ra21, qb1, rb1, rb21))
    ):
        sums.append(
            (
                Sum(2 * n, q_a, r_a, r2_a, z, z_dev, lead_y, y, y_dev),
                Sum(2 * n + 1, q_b, r_b, r2_b, y, y_dev, lead_z, z, z_dev),
            )
        )

    for (a, b), (first, width) in zip(sums, PARTS):

        @pl.loop(0, 8)
        def _(i):
            turn, which = lax.div(i, 2), lax.rem(i, 2)
            by = jnp.where(turn == 0, 2, jnp.where(turn == 1, -s, jnp.where(turn == 2, s, 0)))
            p = 2 * step(z, by) + lax.rem(lead_y + which, 2)
            low, high = unit(p, first, width)
            a.q[p, 0] = low
            a.q[p, 1] = high
            pair = lax.rem(lead_y + lax.div(i, 4), 2)
            plane = lax.rem(2 * lead_z + lax.rem(i, 4), RING)
            for n in range(2):
                pl.when(i == n)(lambda n=n: a.long(n))
                pl.when(i == 2 + n)(lambda n=n: a.plain(n))
            low, high = unit(2 * plane + pair, HALF + first, width)
            b.q[4 * pair + lax.div(plane, 2), lax.rem(plane, 2)] = low
            b.q[4 * pair + 2 + lax.div(plane, 2), lax.rem(plane, 2)] = high
            for n in range(2):
                pl.when(i == 1 + 2 * n)(lambda n=n: b.long(n))
                pl.when(i == 5 + 2 * n)(lambda n=n: b.plain(n))

    for pair in sums:
        for i in range(2):
            for part in pair:
                part.middle(i)
    for pair in sums:
        for i in range(2):
            for part in pair:
                part.own(i)
                if i == 0:
                    part.long2()
        for part in pair:
            part.plain2()
    for pair in sums:
        for part in pair:
            part.middle2()
    for (a, b), (first, width) in zip(sums, PARTS):
        a.finish(slice(first, first + width))
        b.finish(slice(HALF + first, HALF + first + width))

    done(v.at[pl.ds(0, 7 * ROWS)], v_send.at[0])
    done(k.at[pl.ds(0, 7 * CAP)], k_send.at[0])
    for n in range(CHUNKS):
        done(p_slots(n, 15), p_send.at[n])
    done(st.at[pl.ds(0, GROUPS - 1)], s_send.at[0])
    for pair in sums:
        for part in pair:
            part.sent()


def per_device(visual, projector, key_weight, norm_gain, cotangent, residual, counts, offsets):
    anywhere = pl.BlockSpec(memory_space=pl.ANY)
    scalars = pl.BlockSpec(memory_space=pltpu.SMEM)
    dma = pltpu.SemaphoreType.DMA
    return pl.pallas_call(
        kernel,
        out_shape=(
            pltpu.VMEM((BLOCK, WIDTH), F32),
            pltpu.VMEM((ENC, WIDTH), BF16),
        ),
        in_specs=[
            anywhere, anywhere, anywhere, anywhere, anywhere, anywhere, scalars, scalars,
        ],
        out_specs=(pl.BlockSpec(memory_space=pltpu.VMEM),) * 2,
        scratch_shapes=[
            pltpu.VMEM((ALL_ROWS, ENC), BF16),
            pltpu.VMEM((ENC, ALL_ROWS), BF16),
            pltpu.VMEM((2, 16, BLOCK, WIDE), BF16),
            pltpu.VMEM((2, 16, BLOCK, NARROW), BF16),
            pltpu.VMEM((ENC, 2 * WIDE), BF16),
            pltpu.VMEM((ALL_ROWS, WIDTH), BF16),
            pltpu.VMEM((ALL_ROWS, WIDTH), F32),
            pltpu.VMEM((GROUPS * CAP, TROWS, KEYS), BF16),
            pltpu.VMEM((ALL_ROWS, KEYS), BF16),
            pltpu.VMEM((WIDTH, KEYS), BF16),
            pltpu.VMEM((512, KEYS), BF16),
            pltpu.VMEM((SLOT_ROWS, 512), BF16),
            pltpu.VMEM((ALL_ROWS, WIDTH), BF16),
            pltpu.VMEM((WIDTH,), BF16),
            pltpu.VMEM((GROUPS, 2 * GROUPS, 128), F32),
            *[pltpu.VMEM((8, 2, BLOCK, w), BF16) for _, w in PARTS],
            *[pltpu.VMEM((8, 2, BLOCK, w), BF16) for _, w in PARTS],
            *[pltpu.VMEM((6, 2, BLOCK, w), BF16) for _, w in PARTS],
            *[pltpu.VMEM((6, 2, BLOCK, w), BF16) for _, w in PARTS],
            *[pltpu.VMEM((3, BLOCK, w), BF16) for _, w in PARTS],
            *[pltpu.VMEM((3, BLOCK, w), BF16) for _, w in PARTS],
            dma((9,)),
            dma((1,)), dma((3, ROW_PIECES)), dma((4,)),
            dma((1,)), dma((3, KEY_PIECES)), dma((4,)),
            dma((CHUNKS,)), dma((CHUNKS, 7)), dma((CHUNKS,)), dma((1,)), dma((1,)),
            dma((4,)), dma((4, 2)), dma((4, 2)), dma((4,)), dma((4,)), dma((4,)),
        ],
        compiler_params=pltpu.CompilerParams(
            collective_id=0, has_side_effects=True, vmem_limit_bytes=54 * 2**20
        ),
        cost_estimate=pl.CostEstimate(flops=16 * 10**9, bytes_accessed=20 * 10**6, transcendentals=0),
    )(
        visual[0], projector, key_weight, norm_gain, cotangent[0], residual, counts[0], offsets[0]
    )


def solution(mesh):
    placed = (
        P("dp", "grp", None),
        P("dp", "grp"),
        P(),
        P(),
        P("dp", "grp", None),
        P("dp", "grp"),
        P("dp", None, None),
        P("dp", None, None),
    )
    return jax.shard_map(
        per_device,
        mesh=mesh,
        in_specs=placed,
        out_specs=(P("dp", "grp"), P("dp", "grp")),
        check_vma=False,
    )
```

```python
import jax
import jax.numpy as jnp
from jax import lax
from jax.experimental import pallas as pl
from jax.experimental.pallas import tpu as pltpu
from jax.sharding import PartitionSpec as P

MESH = pl.DeviceIdType.MESH
F32 = jnp.float32
BF16 = jnp.bfloat16

norm_eps = 1e-06
clip_limit = 0.5

RING = 4
GROUPS = 8
TROWS = 32
TILES = 4
CAP = 8
ROWS = 128
ALL_ROWS = GROUPS * ROWS
ENC = 3200
BLOCK = 200
PAIR = 2 * BLOCK
WIDTH = 1024
HALF = WIDTH // 2
PARTS = ((0, 384), (384, 128))
KEYS = 512
SLOT_ROWS = CAP * TROWS
CHUNKS = 4
WIDE, NARROW = 384, 128
ROW_PIECES, KEY_PIECES = 4, 2
WRITES = 8


def kernel(
    visual, projector, key_weight, gain, cotangent, residual, counts, offsets,
    wg, res,
    v, vt, wide, narrow, pf, yv, uk, k, kw, cot, onehot, rg, gains, st,
    qa0, qa1, qb0, qb1, ra0, ra1, rb0, rb1, ra20, ra21, rb20, rb21,
    local_sem,
    v_send, v_recv, v_other, k_send, k_recv, k_other, p_send, p_recv, p_end, s_send, s_recv,
    q_send, q_long, q_near, q2_send, q2_long, q2_near,
):
    g, d = lax.axis_index("grp"), lax.axis_index("dp")
    x, c = lax.div(g, 2), lax.rem(g, 2)
    z, y = lax.div(d, RING), lax.rem(d, RING)
    s = 1 - 2 * c

    def step(at, n):
        return lax.rem(at + n + 2 * RING, RING)

    def grp_dev(n):
        return (step(x, n) * 2 + c, d)

    other = (x * 2 + 1 - c, d)

    def y_dev(n):
        return (g, z * RING + step(y, n))

    def z_dev(n):
        return (g, step(z, n) * RING + y)

    def remote(src, dst, send, recv, device):
        return pltpu.make_async_remote_copy(
            src, dst, send, recv, device_id=device, device_id_type=MESH
        )

    def start(src, dst, send, recv, device):
        remote(src, dst, send, recv, device).start()

    def done(like, sem):
        pltpu.make_async_copy(like, like, sem).wait()

    own_rows = pl.ds(pl.multiple_of(g * ROWS, ROWS), ROWS)
    loads = [
        pltpu.make_async_copy(visual, v.at[own_rows], local_sem.at[0]),
        pltpu.make_async_copy(cotangent, cot, local_sem.at[1]),
        pltpu.make_async_copy(
            key_weight.at[pl.ds(pl.multiple_of(g * WIDTH, WIDTH), WIDTH)], kw, local_sem.at[2]
        ),
        pltpu.make_async_copy(residual, res, local_sem.at[3]),
    ]

    def chunk_cols(n):
        return (n * WIDE, WIDE) if n < 2 else (2 * WIDE + (n - 2) * NARROW, NARROW)

    def pj(n, slot):
        return wide.at[n, slot] if n < 2 else narrow.at[n - 2, slot]

    for n in range(CHUNKS):
        loads.append(
            pltpu.make_async_copy(
                projector.at[:, pl.ds(*chunk_cols(n))], pj(n, d), local_sem.at[4 + n]
            )
        )
    loads.append(
        pltpu.make_async_copy(
            gain.at[pl.ds(pl.multiple_of(g * WIDTH, WIDTH), WIDTH)], gains, local_sem.at[8]
        )
    )
    for load in loads:
        load.start()

    barrier = pltpu.get_barrier_semaphore()
    friends = [(lax.rem(g + n, GROUPS), d) for n in range(1, GROUPS)]
    friends += [y_dev(n) for n in (1, 2, 3)] + [z_dev(n) for n in (1, 2, 3)]
    for friend in friends:
        pl.semaphore_signal(barrier, inc=1, device_id=friend, device_id_type=MESH)
    pl.semaphore_wait(barrier, len(friends))

    def x_slot(n, core):
        return step(x, n) * 2 + core

    class Gather:
        def __init__(self, buf, rows, pieces, send, recv, other_recv):
            self.buf, self.rows, self.send, self.recv = buf, rows, send, recv
            self.other = other_recv
            self.pieces, self.piece = pieces, rows // pieces

        def at(self, slot, i):
            row = pl.multiple_of(slot * self.rows + i * self.piece, self.piece)
            return self.buf.at[pl.ds(row, self.piece)]

        def go(self, m, i, slot, device):
            here = self.at(slot, i)
            start(here, here, self.send, self.recv.at[m, i], device)

        def give(self, m, i, slot):
            here = self.at(slot, i)
            start(here, here, self.send, self.other.at[m], other)

        def own(self, i):
            self.go(0, i, g, grp_dev(s))
            self.go(1, i, g, grp_dev(-s))

        def own_other(self, i):
            self.give(0, i, g)

        def near(self, i):
            done(self.at(x_slot(-s, c), i), self.recv.at[0, i])
            self.go(2, i, x_slot(-s, c), grp_dev(s))
            self.give(1, i, x_slot(-s, c))
            done(self.at(x_slot(s, c), i), self.recv.at[1, i])
            self.give(2, i, x_slot(s, c))

        def far(self, i):
            done(self.at(x_slot(2, c), i), self.recv.at[2, i])
            self.give(3, i, x_slot(2, c))

        def from_other(self, m):
            done(self.buf.at[pl.ds(0, self.rows)], self.other.at[m])

    rows = Gather(v, ROWS, ROW_PIECES, v_send.at[0], v_recv, v_other)
    keys = Gather(k, CAP, KEY_PIECES, k_send.at[0], k_recv, k_other)

    loads[0].wait()
    for i in range(ROW_PIECES):
        rows.own(i)

    def p_slot(n, first, second):
        if n % 2 == 0:
            return step(z, second) * RING + step(y, first)
        return step(z, first) * RING + step(y, second)

    def p_go(n, recv, slot, device):
        start(pj(n, slot), pj(n, slot), p_send.at[n], recv, device)

    def p_wait(n, m, slot):
        done(pj(n, slot), p_recv.at[n, m])

    def first_dev(n, by):
        return y_dev(by) if n % 2 == 0 else z_dev(by)

    def second_dev(n, by):
        return z_dev(by) if n % 2 == 0 else y_dev(by)

    firsts = (0, -s, s, 2)

    def p_spread(n, j):
        slot = p_slot(n, firsts[j], 0)
        p_go(n, p_recv.at[n, 3 + j], slot, second_dev(n, s))
        p_go(n, p_end.at[n], slot, second_dev(n, -s))

    def p_own(n):
        p_go(n, p_recv.at[n, 0], d, first_dev(n, s))
        p_go(n, p_recv.at[n, 1], d, first_dev(n, -s))

    def p_first(n):
        p_wait(n, 0, p_slot(n, -s, 0))
        p_go(n, p_recv.at[n, 2], p_slot(n, -s, 0), first_dev(n, s))

    def p_first_spread(n):
        p_spread(n, 1)
        p_wait(n, 1, p_slot(n, s, 0))
        p_spread(n, 2)
        p_wait(n, 2, p_slot(n, 2, 0))
        p_spread(n, 3)

    def p_second(n, j):
        p_wait(n, 3 + j, p_slot(n, firsts[j], -s))
        p_go(n, p_end.at[n], p_slot(n, firsts[j], -s), second_dev(n, s))

    def p_slots(n, count):
        return wide.at[n, pl.ds(0, count)] if n < 2 else narrow.at[n - 2, pl.ds(0, count)]

    def p_last(n):
        done(p_slots(n, 8), p_end.at[n])

    for n in range(CHUNKS):
        loads[4 + n].wait()
        p_own(n)
    for n in range(CHUNKS):
        p_spread(n, 0)

    tiles = []
    earlier = [jnp.int32(0)] * GROUPS
    for source in range(GROUPS):
        route = [counts[source, b] for b in range(GROUPS)]
        first = [offsets[source, b] for b in range(GROUPS)]
        for t in range(TILES):
            target, slot, position = jnp.int32(0), jnp.int32(0), jnp.int32(0)
            passed = jnp.int32(0)
            for b in range(GROUPS):
                hit = (passed <= t) & (t < passed + route[b])
                within = t - passed
                target = jnp.where(hit, b, target)
                slot = jnp.where(hit, earlier[b] + within, slot)
                position = jnp.where(hit, first[b] + within * TROWS, position)
                passed = passed + route[b]
            slot = jnp.clip(slot, 0, CAP - 1)
            tiles.append((target, slot, position))
        earlier = [e + r for e, r in zip(earlier, route)]
    slot_iota = (
        lax.broadcasted_iota(jnp.int32, (TROWS, KEYS), 1)
        - lax.broadcasted_iota(jnp.int32, (TROWS, KEYS), 0)
    )
    for i in range(CAP):
        place = jnp.int32(-4096)
        for target, slot, position in tiles:
            place = jnp.where((target == g) & (slot == i), position, place)
        onehot[i * TROWS : (i + 1) * TROWS, :] = jnp.where(slot_iota == place, 1.0, 0.0).astype(BF16)
    loads[1].wait()
    k[pl.ds(g * CAP, CAP)] = jnp.dot(
        onehot[...], cot[...], preferred_element_type=F32
    ).astype(BF16).reshape(CAP, TROWS, KEYS)
    def transpose(slot):
        @pl.loop(0, 5)
        def _(i):
            cols = pl.ds(pl.multiple_of(i * 640, 640), 640)
            block = v[pl.ds(pl.multiple_of(slot * ROWS, ROWS), ROWS), cols]
            vt[cols, pl.ds(pl.multiple_of(slot * ROWS, ROWS), ROWS)] = block.T

    def assemble(pair):
        bufs, width = ((wide, WIDE), (narrow, NARROW))[pair]

        @pl.loop(0, 8)
        def _(i):
            part = pl.ds(pl.multiple_of(i * PAIR, PAIR), PAIR)
            for n in range(2):
                both = [bufs[n, 2 * i].astype(F32), bufs[n, 2 * i + 1].astype(F32)]
                pf[part, n * width : (n + 1) * width] = jnp.concatenate(both, axis=0).astype(BF16)

    def project(pair, row, count):
        first, last = ((0, 2 * WIDE), (2 * WIDE, WIDTH))[pair]
        part = pl.ds(pl.multiple_of(row, 2 * ROWS), count)
        yv[part, first:last] = jnp.dot(
            v[part, :], pf[:, : last - first], preferred_element_type=F32
        ).astype(BF16)

    def project_chip(by):
        project(0, step(x, by) * 2 * ROWS, 2 * ROWS)

    def key_side(slot):
        part = pl.ds(slot * CAP, CAP)
        product = lax.dot_general(
            k[part].reshape(SLOT_ROWS, KEYS), kw[...], (((1,), (1,)), ((), ())),
            preferred_element_type=F32,
        )
        uk[part] = (gains[...].astype(F32).reshape(1, WIDTH) * product).reshape(CAP, TROWS, WIDTH)

    for n in (0, 1):
        p_first(n)
    for i in range(ROW_PIECES):
        rows.own_other(i)
    for n in (2, 3):
        p_first(n)
    for n in (0, 1):
        p_first_spread(n)
    rows.near(0)
    for n in (2, 3):
        p_first_spread(n)
    transpose(g)
    for n in (0, 1):
        p_second(n, 0)
    rows.near(1)
    rows.from_other(0)
    transpose(x_slot(0, 1 - c))
    rows.near(2)
    for i in range(KEY_PIECES):
        keys.own(i)
        keys.own_other(i)
    for n in (0, 1):
        p_second(n, 1)
    rows.near(3)
    loads[2].wait()
    loads[8].wait()
    key_side(g)
    for n in (0, 1):
        p_second(n, 2)
    transpose(x_slot(-s, c))
    rows.far(0)
    transpose(x_slot(s, c))
    rows.far(1)
    for n in (0, 1):
        p_second(n, 3)
    rows.from_other(1)
    transpose(x_slot(s, 1 - c))
    rows.far(2)
    for n in (2, 3):
        p_second(n, 0)
    rows.from_other(2)
    transpose(x_slot(-s, 1 - c))
    rows.far(3)
    for n in (2, 3):
        p_second(n, 1)
    keys.from_other(0)
    key_side(x_slot(0, 1 - c))
    for n in (2, 3):
        p_second(n, 2)
    for n in (0, 1):
        p_last(n)
    assemble(0)
    keys.near(0)
    project_chip(0)
    for n in (2, 3):
        p_second(n, 3)
    keys.near(1)
    project_chip(-s)
    project_chip(s)
    keys.from_other(1)
    key_side(x_slot(s, 1 - c))
    rows.from_other(3)
    keys.far(0)
    project_chip(2)
    key_side(x_slot(-s, c))
    key_side(x_slot(s, c))
    keys.from_other(2)
    key_side(x_slot(-s, 1 - c))
    keys.far(1)
    for n in (2, 3):
        p_last(n)
    assemble(1)
    project(1, 0, 512)
    project(1, 512, 512)
    key_side(x_slot(2, c))
    keys.from_other(3)
    key_side(x_slot(2, 1 - c))

    for i in range(GROUPS):
        sums = []
        for n in range(i * TILES, (i + 1) * TILES):
            target, slot, _ = tiles[n]
            side = uk[target * CAP + slot]
            squares = jnp.zeros((TROWS, 128), F32)
            products = jnp.zeros((TROWS, 128), F32)
            for j in range(WIDTH // 128):
                cols = slice(j * 128, (j + 1) * 128)
                value = yv[n * TROWS : (n + 1) * TROWS, cols].astype(F32)
                squares += value * value
                products += value * side[:, cols]
            sums.append((squares, products))
        for m in range(2):
            block = jnp.concatenate([pair[m] for pair in sums], axis=0)
            st[g, pl.ds(m * GROUPS + i, 1), :] = jnp.sum(block.T, axis=0, keepdims=True)
    for n in range(1, GROUPS):
        start(st.at[g], st.at[g], s_send.at[0], s_recv.at[0], (lax.rem(g + n, GROUPS), d))
    transpose(x_slot(2, c))
    transpose(x_slot(2, 1 - c))
    done(st.at[pl.ds(0, GROUPS - 1)], s_recv.at[0])
    total = st[0]
    for n in range(1, GROUPS):
        total = total + st[n]
    mean = total * (1.0 / (GROUPS * WIDTH))
    inverse = lax.rsqrt(mean[:GROUPS] + norm_eps)
    inner = inverse * mean[GROUPS:]
    for i in range(GROUPS):
        inv = jnp.broadcast_to(inverse[i : i + 1], (ROWS, 128)).T
        inn = jnp.broadcast_to((inverse * inner)[i : i + 1], (ROWS, 128)).T
        for n in range(TILES):
            target, slot, _ = tiles[i * TILES + n]
            side = uk[target * CAP + slot]
            here = slice(n * TROWS, (n + 1) * TROWS)
            rows_here = slice((i * TILES + n) * TROWS, (i * TILES + n + 1) * TROWS)
            for j in range(WIDTH // 128):
                cols = slice(j * 128, (j + 1) * 128)
                value = yv[rows_here, cols].astype(F32)
                rg[rows_here, cols] = (inv[here] * (side[:, cols] - value * inn[here])).astype(BF16)

    loads[3].wait()
    lead_y = 1 - lax.div(y, 2)
    lead_z = 1 - lax.div(z, 2)

    def unit(p, first, width):
        part = pl.ds(pl.multiple_of(p * PAIR, PAIR), PAIR)
        cols = slice(first, first + width)
        term = jnp.dot(vt[part, :], rg[:, cols], preferred_element_type=F32)
        carried = term + res[part, cols].astype(F32)
        clipped = jnp.clip(carried, -clip_limit, clip_limit)
        res[part, cols] = (carried - clipped).astype(BF16)
        return clipped[:BLOCK].astype(BF16), clipped[BLOCK:].astype(BF16)

    class Sum:
        def __init__(self, n, q, r, r2, at, near, lead, at2, near2):
            self.n, self.q, self.r, self.r2 = n, q, r, r2
            self.at, self.near, self.lead, self.at2, self.near2 = at, near, lead, at2, near2

        def piece(self, by, i):
            return 2 * step(self.at, by) + lax.rem(self.lead + i, 2)

        def send(self, m, i, by, to):
            recv = q_long.at[self.n, i] if m == 0 else q_near.at[self.n, i]
            start(
                self.q.at[self.piece(by, i)], self.r.at[2 * i + m - 1 if m else 4 + i],
                q_send.at[self.n], recv, self.near(to),
            )

        def long(self, i):
            self.send(0, i, 2, s)

        def long_block(self, i, j):
            start(
                self.q.at[self.piece(2, i), j], self.r.at[4 + i, j],
                q_send.at[self.n], q_long.at[self.n, i], self.near(s),
            )

        def plain(self, i):
            self.send(1, i, -s, -s)

        def middle(self, i):
            done(self.r.at[4 + i], q_long.at[self.n, i])
            self.add(self.piece(s, i), (4 + i,))
            self.send(2, i, s, s)

        def own(self, i):
            done(self.r.at[pl.ds(2 * i, 2)], q_near.at[self.n, i])
            self.add(self.piece(0, i), (2 * i, 2 * i + 1))

        def add(self, index, terms):
            for j in range(2):
                value = self.q[index, j].astype(F32)
                for term in terms:
                    value = value + self.r[term, j].astype(F32)
                self.q[index, j] = value.astype(BF16)

        def block(self, by):
            at2 = step(self.at2, by)
            return (2 * self.at + lax.div(at2, 2), lax.rem(at2, 2))

        def send2(self, m, by, to):
            recv = q2_long.at[self.n] if m == 0 else q2_near.at[self.n]
            start(
                self.q.at[self.block(by)], self.r2.at[(2, 0, 1)[m]],
                q2_send.at[self.n], recv, self.near2(to),
            )

        def long2(self):
            self.send2(0, 2, s)

        def plain2(self):
            self.send2(1, -s, -s)

        def middle2(self):
            done(self.r2.at[2], q2_long.at[self.n])
            here = self.block(s)
            self.q[here] = (self.q[here].astype(F32) + self.r2[2].astype(F32)).astype(BF16)
            self.send2(2, s, s)

        def direct2(self):
            for m in range(1, RING):
                start(
                    self.q.at[self.block(m)], self.r2.at[m - 1],
                    q2_send.at[self.n], q2_near.at[self.n], self.near2(m),
                )

        def finish_direct(self, cols):
            done(self.r2, q2_near.at[self.n])
            total = self.q[self.block(0)].astype(F32)
            for m in range(RING - 1):
                total = total + self.r2[m].astype(F32)
            wg[:, cols] = total

        def finish(self, cols):
            done(self.r2.at[pl.ds(0, 2)], q2_near.at[self.n])
            total = self.q[self.block(0)].astype(F32) + self.r2[0].astype(F32)
            wg[:, cols] = total + self.r2[1].astype(F32)

        def sent(self):
            done(self.r, q_send.at[self.n])
            done(self.r2, q2_send.at[self.n])

    sums = []
    for n, (q_a, r_a, r2_a, q_b, r_b, r2_b) in enumerate(
        ((qa0, ra0, ra20, qb0, rb0, rb20), (qa1, ra1, ra21, qb1, rb1, rb21))
    ):
        sums.append(
            (
                Sum(2 * n, q_a, r_a, r2_a, z, z_dev, lead_y, y, y_dev),
                Sum(2 * n + 1, q_b, r_b, r2_b, y, y_dev, lead_z, z, z_dev),
            )
        )

    def turns(n, begin, end):
        (a, b), (first, width) = sums[n], PARTS[n]

        @pl.loop(begin, end)
        def _(i):
            turn, which = lax.div(i, 2), lax.rem(i, 2)
            by = jnp.where(turn == 0, 2, jnp.where(turn == 1, -s, jnp.where(turn == 2, s, 0)))
            p = 2 * step(z, by) + lax.rem(lead_y + which, 2)
            low, high = unit(p, first, width)
            a.q[p, 0] = low
            a.q[p, 1] = high
            pair = lax.rem(lead_y + lax.div(i, 4), 2)
            plane = lax.rem(2 * lead_z + lax.rem(i, 4), RING)
            for n in range(2):
                pl.when(i == n)(lambda n=n: a.long(n))
                pl.when(i == 2 + n)(lambda n=n: a.plain(n))
            low, high = unit(2 * plane + pair, HALF + first, width)
            b.q[4 * pair + lax.div(plane, 2), lax.rem(plane, 2)] = low
            b.q[4 * pair + 2 + lax.div(plane, 2), lax.rem(plane, 2)] = high
            for n in range(2):
                pl.when(i == 5 + 2 * n)(lambda n=n: b.plain(n))
            for n in range(4):
                pl.when(i == n)(lambda n=n: b.long_block(n // 2, n % 2))

    def middles(n, i):
        for part in sums[n]:
            part.middle(i)

    turns(0, 0, 8)
    turns(1, 0, 4)
    middles(0, 0)
    turns(1, 4, 8)
    middles(0, 1)
    middles(1, 0)
    middles(1, 1)
    early, late = sums
    for i in range(2):
        for part in early:
            part.own(i)
            if i == 0:
                part.long2()
    for part in early:
        part.plain2()
    for part in early:
        part.middle2()
    for i in range(2):
        for part in late:
            part.own(i)
    for part in late:
        part.direct2()
    for pair, (first, width) in zip(sums, PARTS):
        for n, part in enumerate(pair):
            cols = slice(n * HALF + first, n * HALF + first + width)
            part.finish(cols) if pair is early else part.finish_direct(cols)

    done(v.at[pl.ds(0, 7 * ROWS)], v_send.at[0])
    done(k.at[pl.ds(0, 7 * CAP)], k_send.at[0])
    for n in range(CHUNKS):
        done(p_slots(n, 15), p_send.at[n])
    done(st.at[pl.ds(0, GROUPS - 1)], s_send.at[0])
    for pair in sums:
        for part in pair:
            part.sent()


def write_back(grad, left, grad_out, left_out, sems):
    copies = []
    for i in range(WRITES):
        part = pl.ds(i * (ENC // WRITES), ENC // WRITES)
        copies.append(pltpu.make_async_copy(left.at[part], left_out.at[part], sems.at[i]))
    copies.append(pltpu.make_async_copy(grad, grad_out, sems.at[WRITES]))
    for copy in copies:
        copy.start()
    for copy in copies:
        copy.wait()


def per_device(visual, projector, key_weight, norm_gain, cotangent, residual, counts, offsets):
    anywhere = pl.BlockSpec(memory_space=pl.ANY)
    scalars = pl.BlockSpec(memory_space=pltpu.SMEM)
    dma = pltpu.SemaphoreType.DMA
    results = pl.pallas_call(
        kernel,
        out_shape=(
            pltpu.VMEM((BLOCK, WIDTH), F32),
            pltpu.VMEM((ENC, WIDTH), BF16),
        ),
        in_specs=[
            anywhere, anywhere, anywhere, anywhere, anywhere, anywhere, scalars, scalars,
        ],
        out_specs=(pl.BlockSpec(memory_space=pltpu.VMEM),) * 2,
        scratch_shapes=[
            pltpu.VMEM((ALL_ROWS, ENC), BF16),
            pltpu.VMEM((ENC, ALL_ROWS), BF16),
            pltpu.VMEM((2, 16, BLOCK, WIDE), BF16),
            pltpu.VMEM((2, 16, BLOCK, NARROW), BF16),
            pltpu.VMEM((ENC, 2 * WIDE), BF16),
            pltpu.VMEM((ALL_ROWS, WIDTH), BF16),
            pltpu.VMEM((GROUPS * CAP, TROWS, WIDTH), F32),
            pltpu.VMEM((GROUPS * CAP, TROWS, KEYS), BF16),
            pltpu.VMEM((WIDTH, KEYS), BF16),
            pltpu.VMEM((512, KEYS), BF16),
            pltpu.VMEM((SLOT_ROWS, 512), BF16),
            pltpu.VMEM((ALL_ROWS, WIDTH), BF16),
            pltpu.VMEM((WIDTH,), BF16),
            pltpu.VMEM((GROUPS, 2 * GROUPS, 128), F32),
            *[pltpu.VMEM((8, 2, BLOCK, w), BF16) for _, w in PARTS],
            *[pltpu.VMEM((8, 2, BLOCK, w), BF16) for _, w in PARTS],
            *[pltpu.VMEM((6, 2, BLOCK, w), BF16) for _, w in PARTS],
            *[pltpu.VMEM((6, 2, BLOCK, w), BF16) for _, w in PARTS],
            *[pltpu.VMEM((3, BLOCK, w), BF16) for _, w in PARTS],
            *[pltpu.VMEM((3, BLOCK, w), BF16) for _, w in PARTS],
            dma((9,)),
            dma((1,)), dma((3, ROW_PIECES)), dma((4,)),
            dma((1,)), dma((3, KEY_PIECES)), dma((4,)),
            dma((CHUNKS,)), dma((CHUNKS, 7)), dma((CHUNKS,)), dma((1,)), dma((1,)),
            dma((4,)), dma((4, 2)), dma((4, 2)), dma((4,)), dma((4,)), dma((4,)),
        ],
        compiler_params=pltpu.CompilerParams(
            collective_id=0, has_side_effects=True, vmem_limit_bytes=56 * 2**20
        ),
        cost_estimate=pl.CostEstimate(flops=16 * 10**9, bytes_accessed=20 * 10**6, transcendentals=0),
    )(
        visual[0], projector, key_weight, norm_gain, cotangent[0], residual, counts[0], offsets[0]
    )
    grad, left = [pltpu.with_memory_space_constraint(r, pltpu.VMEM) for r in results]
    return pl.pallas_call(
        write_back,
        out_shape=(
            jax.ShapeDtypeStruct((BLOCK, WIDTH), F32),
            jax.ShapeDtypeStruct((ENC, WIDTH), BF16),
        ),
        in_specs=[pl.BlockSpec(memory_space=pltpu.VMEM)] * 2,
        out_specs=(anywhere, anywhere),
        scratch_shapes=[dma((WRITES + 1,))],
        compiler_params=pltpu.CompilerParams(vmem_limit_bytes=2**20),
    )(grad, left)


def solution(mesh):
    placed = (
        P("dp", "grp", None),
        P("dp", "grp"),
        P(),
        P(),
        P("dp", "grp", None),
        P("dp", "grp"),
        P("dp", None, None),
        P("dp", None, None),
    )
    return jax.shard_map(
        per_device,
        mesh=mesh,
        in_specs=placed,
        out_specs=(P("dp", "grp"), P("dp", "grp")),
        check_vma=False,
    )
```

```python
import jax
import jax.numpy as jnp
from jax import lax
from jax.experimental import pallas as pl
from jax.experimental.pallas import tpu as pltpu
from jax.sharding import PartitionSpec as P

MESH = pl.DeviceIdType.MESH
F32 = jnp.float32
BF16 = jnp.bfloat16

norm_eps = 1e-06
clip_limit = 0.5

RING = 4
GROUPS = 8
TROWS = 32
TILES = 4
CAP = 8
ROWS = 128
ALL_ROWS = GROUPS * ROWS
ENC = 3200
BLOCK = 200
PAIR = 2 * BLOCK
WIDTH = 1024
HALF = WIDTH // 2
PARTS = ((0, 384), (384, 128))
KEYS = 512
SLOT_ROWS = CAP * TROWS
CHUNKS = 4
WIDE, NARROW = 384, 128
ROW_PIECES, KEY_PIECES = 4, 2
WRITES = 8


def kernel(
    visual, projector, key_weight, gain, cotangent, residual, counts, offsets,
    wg, res,
    v, vt, wide, narrow, pf, yv, uk, k, kw, cot, onehot, rg, gains, st,
    qa0, qa1, qb0, qb1, ra0, ra1, rb0, rb1, ra20, ra21, rb20, rb21,
    local_sem,
    v_send, v_recv, v_other, k_send, k_recv, k_other, p_send, p_recv, p_end, s_send, s_recv,
    q_send, q_long, q_near, q2_send, q2_long, q2_near,
):
    g, d = lax.axis_index("grp"), lax.axis_index("dp")
    x, c = lax.div(g, 2), lax.rem(g, 2)
    z, y = lax.div(d, RING), lax.rem(d, RING)
    s = 1 - 2 * c

    def step(at, n):
        return lax.rem(at + n + 2 * RING, RING)

    def grp_dev(n):
        return (step(x, n) * 2 + c, d)

    other = (x * 2 + 1 - c, d)

    def y_dev(n):
        return (g, z * RING + step(y, n))

    def z_dev(n):
        return (g, step(z, n) * RING + y)

    def remote(src, dst, send, recv, device):
        return pltpu.make_async_remote_copy(
            src, dst, send, recv, device_id=device, device_id_type=MESH
        )

    def start(src, dst, send, recv, device):
        remote(src, dst, send, recv, device).start()

    def done(like, sem):
        pltpu.make_async_copy(like, like, sem).wait()

    own_rows = pl.ds(pl.multiple_of(g * ROWS, ROWS), ROWS)
    loads = [
        pltpu.make_async_copy(visual, v.at[own_rows], local_sem.at[0]),
        pltpu.make_async_copy(cotangent, cot, local_sem.at[1]),
        pltpu.make_async_copy(
            key_weight.at[pl.ds(pl.multiple_of(g * WIDTH, WIDTH), WIDTH)], kw, local_sem.at[2]
        ),
        pltpu.make_async_copy(residual, res, local_sem.at[3]),
    ]

    def chunk_cols(n):
        return (n * WIDE, WIDE) if n < 2 else (2 * WIDE + (n - 2) * NARROW, NARROW)

    def pj(n, slot):
        return wide.at[n, slot] if n < 2 else narrow.at[n - 2, slot]

    for n in range(CHUNKS):
        loads.append(
            pltpu.make_async_copy(
                projector.at[:, pl.ds(*chunk_cols(n))], pj(n, d), local_sem.at[4 + n]
            )
        )
    loads.append(
        pltpu.make_async_copy(
            gain.at[pl.ds(pl.multiple_of(g * WIDTH, WIDTH), WIDTH)], gains, local_sem.at[8]
        )
    )
    for load in loads:
        load.start()

    barrier = pltpu.get_barrier_semaphore()
    friends = [(lax.rem(g + n, GROUPS), d) for n in range(1, GROUPS)]
    friends += [y_dev(n) for n in (1, 2, 3)] + [z_dev(n) for n in (1, 2, 3)]
    for friend in friends:
        pl.semaphore_signal(barrier, inc=1, device_id=friend, device_id_type=MESH)
    pl.semaphore_wait(barrier, len(friends))

    def x_slot(n, core):
        return step(x, n) * 2 + core

    class Gather:
        def __init__(self, buf, rows, pieces, send, recv, other_recv):
            self.buf, self.rows, self.send, self.recv = buf, rows, send, recv
            self.other = other_recv
            self.pieces, self.piece = pieces, rows // pieces

        def at(self, slot, i):
            row = pl.multiple_of(slot * self.rows + i * self.piece, self.piece)
            return self.buf.at[pl.ds(row, self.piece)]

        def go(self, m, i, slot, device):
            here = self.at(slot, i)
            start(here, here, self.send, self.recv.at[m, i], device)

        def give(self, m, i, slot):
            here = self.at(slot, i)
            start(here, here, self.send, self.other.at[m], other)

        def own(self, i):
            self.go(0, i, g, grp_dev(s))
            self.go(1, i, g, grp_dev(-s))

        def own_other(self, i):
            self.give(0, i, g)

        def near(self, i):
            done(self.at(x_slot(-s, c), i), self.recv.at[0, i])
            self.go(2, i, x_slot(-s, c), grp_dev(s))
            self.give(1, i, x_slot(-s, c))
            done(self.at(x_slot(s, c), i), self.recv.at[1, i])
            self.give(2, i, x_slot(s, c))

        def far(self, i):
            done(self.at(x_slot(2, c), i), self.recv.at[2, i])
            self.give(3, i, x_slot(2, c))

        def from_other(self, m):
            done(self.buf.at[pl.ds(0, self.rows)], self.other.at[m])

    rows = Gather(v, ROWS, ROW_PIECES, v_send.at[0], v_recv, v_other)
    keys = Gather(k, CAP, KEY_PIECES, k_send.at[0], k_recv, k_other)

    loads[0].wait()
    for i in range(ROW_PIECES):
        rows.own(i)

    def p_slot(n, first, second):
        if n % 2 == 0:
            return step(z, second) * RING + step(y, first)
        return step(z, first) * RING + step(y, second)

    def p_go(n, recv, slot, device):
        start(pj(n, slot), pj(n, slot), p_send.at[n], recv, device)

    def p_wait(n, m, slot):
        done(pj(n, slot), p_recv.at[n, m])

    def first_dev(n, by):
        return y_dev(by) if n % 2 == 0 else z_dev(by)

    def second_dev(n, by):
        return z_dev(by) if n % 2 == 0 else y_dev(by)

    firsts = (0, -s, s, 2)

    def p_spread(n, j):
        slot = p_slot(n, firsts[j], 0)
        p_go(n, p_recv.at[n, 3 + j], slot, second_dev(n, s))
        p_go(n, p_end.at[n], slot, second_dev(n, -s))

    def p_own(n):
        p_go(n, p_recv.at[n, 0], d, first_dev(n, s))
        p_go(n, p_recv.at[n, 1], d, first_dev(n, -s))

    def p_first(n):
        p_wait(n, 0, p_slot(n, -s, 0))
        p_go(n, p_recv.at[n, 2], p_slot(n, -s, 0), first_dev(n, s))

    def p_first_spread(n):
        p_spread(n, 1)
        p_wait(n, 1, p_slot(n, s, 0))
        p_spread(n, 2)
        p_wait(n, 2, p_slot(n, 2, 0))
        p_spread(n, 3)

    def p_second(n, j):
        p_wait(n, 3 + j, p_slot(n, firsts[j], -s))
        p_go(n, p_end.at[n], p_slot(n, firsts[j], -s), second_dev(n, s))

    def p_slots(n, count):
        return wide.at[n, pl.ds(0, count)] if n < 2 else narrow.at[n - 2, pl.ds(0, count)]

    def p_last(n):
        done(p_slots(n, 8), p_end.at[n])

    for n in range(CHUNKS):
        loads[4 + n].wait()
        p_own(n)
    for n in range(CHUNKS):
        p_spread(n, 0)

    tiles = []
    earlier = [jnp.int32(0)] * GROUPS
    for source in range(GROUPS):
        route = [counts[source, b] for b in range(GROUPS)]
        first = [offsets[source, b] for b in range(GROUPS)]
        for t in range(TILES):
            target, slot, position = jnp.int32(0), jnp.int32(0), jnp.int32(0)
            passed = jnp.int32(0)
            for b in range(GROUPS):
                hit = (passed <= t) & (t < passed + route[b])
                within = t - passed
                target = jnp.where(hit, b, target)
                slot = jnp.where(hit, earlier[b] + within, slot)
                position = jnp.where(hit, first[b] + within * TROWS, position)
                passed = passed + route[b]
            slot = jnp.clip(slot, 0, CAP - 1)
            tiles.append((target, slot, position))
        earlier = [e + r for e, r in zip(earlier, route)]
    slot_iota = (
        lax.broadcasted_iota(jnp.int32, (TROWS, KEYS), 1)
        - lax.broadcasted_iota(jnp.int32, (TROWS, KEYS), 0)
    )
    for i in range(CAP):
        place = jnp.int32(-4096)
        for target, slot, position in tiles:
            place = jnp.where((target == g) & (slot == i), position, place)
        onehot[i * TROWS : (i + 1) * TROWS, :] = jnp.where(slot_iota == place, 1.0, 0.0).astype(BF16)
    loads[1].wait()
    k[pl.ds(g * CAP, CAP)] = jnp.dot(
        onehot[...], cot[...], preferred_element_type=F32
    ).astype(BF16).reshape(CAP, TROWS, KEYS)
    def transpose(slot):
        @pl.loop(0, 5)
        def _(i):
            cols = pl.ds(pl.multiple_of(i * 640, 640), 640)
            block = v[pl.ds(pl.multiple_of(slot * ROWS, ROWS), ROWS), cols]
            vt[cols, pl.ds(pl.multiple_of(slot * ROWS, ROWS), ROWS)] = block.T

    def assemble(pair):
        bufs, width = ((wide, WIDE), (narrow, NARROW))[pair]

        @pl.loop(0, 8)
        def _(i):
            part = pl.ds(pl.multiple_of(i * PAIR, PAIR), PAIR)
            for n in range(2):
                both = [bufs[n, 2 * i].astype(F32), bufs[n, 2 * i + 1].astype(F32)]
                pf[part, n * width : (n + 1) * width] = jnp.concatenate(both, axis=0).astype(BF16)

    def project(pair, row, count):
        first, last = ((0, 2 * WIDE), (2 * WIDE, WIDTH))[pair]
        part = pl.ds(pl.multiple_of(row, 2 * ROWS), count)
        yv[part, first:last] = jnp.dot(
            v[part, :], pf[:, : last - first], preferred_element_type=F32
        ).astype(BF16)

    def project_chip(by):
        project(0, step(x, by) * 2 * ROWS, 2 * ROWS)

    def key_side(slot):
        part = pl.ds(slot * CAP, CAP)
        product = lax.dot_general(
            k[part].reshape(SLOT_ROWS, KEYS), kw[...], (((1,), (1,)), ((), ())),
            preferred_element_type=F32,
        )
        uk[part] = (gains[...].astype(F32).reshape(1, WIDTH) * product).reshape(CAP, TROWS, WIDTH)

    for n in (0, 1):
        p_first(n)
    for i in range(ROW_PIECES):
        rows.own_other(i)
    for n in (2, 3):
        p_first(n)
    for n in (0, 1):
        p_first_spread(n)
    rows.near(0)
    for n in (2, 3):
        p_first_spread(n)
    transpose(g)
    for n in (0, 1):
        p_second(n, 0)
    rows.near(1)
    rows.from_other(0)
    transpose(x_slot(0, 1 - c))
    rows.near(2)
    for i in range(KEY_PIECES):
        keys.own(i)
        keys.own_other(i)
    for n in (0, 1):
        p_second(n, 1)
    rows.near(3)
    loads[2].wait()
    loads[8].wait()
    key_side(g)
    for n in (0, 1):
        p_second(n, 2)
    transpose(x_slot(-s, c))
    rows.far(0)
    transpose(x_slot(s, c))
    rows.far(1)
    for n in (0, 1):
        p_second(n, 3)
    rows.from_other(1)
    transpose(x_slot(s, 1 - c))
    rows.far(2)
    for n in (2, 3):
        p_second(n, 0)
    rows.from_other(2)
    transpose(x_slot(-s, 1 - c))
    rows.far(3)
    for n in (2, 3):
        p_second(n, 1)
    keys.from_other(0)
    key_side(x_slot(0, 1 - c))
    for n in (2, 3):
        p_second(n, 2)
    for n in (0, 1):
        p_last(n)
    assemble(0)
    keys.near(0)
    project_chip(0)
    for n in (2, 3):
        p_second(n, 3)
    keys.near(1)
    project_chip(-s)
    project_chip(s)
    keys.from_other(1)
    key_side(x_slot(s, 1 - c))
    rows.from_other(3)
    keys.far(0)
    project_chip(2)
    key_side(x_slot(-s, c))
    key_side(x_slot(s, c))
    keys.from_other(2)
    key_side(x_slot(-s, 1 - c))
    keys.far(1)
    for n in (2, 3):
        p_last(n)
    assemble(1)
    project(1, 0, 512)
    project(1, 512, 512)
    key_side(x_slot(2, c))
    keys.from_other(3)
    key_side(x_slot(2, 1 - c))

    for i in range(GROUPS):
        sums = []
        for n in range(i * TILES, (i + 1) * TILES):
            target, slot, _ = tiles[n]
            side = uk[target * CAP + slot]
            squares = jnp.zeros((TROWS, 128), F32)
            products = jnp.zeros((TROWS, 128), F32)
            for j in range(WIDTH // 128):
                cols = slice(j * 128, (j + 1) * 128)
                value = yv[n * TROWS : (n + 1) * TROWS, cols].astype(F32)
                squares += value * value
                products += value * side[:, cols]
            sums.append((squares, products))
        for m in range(2):
            block = jnp.concatenate([pair[m] for pair in sums], axis=0)
            st[g, pl.ds(m * GROUPS + i, 1), :] = jnp.sum(block.T, axis=0, keepdims=True)
    for n in range(1, GROUPS):
        start(st.at[g], st.at[g], s_send.at[0], s_recv.at[0], (lax.rem(g + n, GROUPS), d))
    transpose(x_slot(2, c))
    transpose(x_slot(2, 1 - c))
    done(st.at[pl.ds(0, GROUPS - 1)], s_recv.at[0])
    total = st[0]
    for n in range(1, GROUPS):
        total = total + st[n]
    mean = total * (1.0 / (GROUPS * WIDTH))
    inverse = lax.rsqrt(mean[:GROUPS] + norm_eps)
    inner = inverse * mean[GROUPS:]
    for i in range(GROUPS):
        inv = jnp.broadcast_to(inverse[i : i + 1], (ROWS, 128)).T
        inn = jnp.broadcast_to((inverse * inner)[i : i + 1], (ROWS, 128)).T
        for n in range(TILES):
            target, slot, _ = tiles[i * TILES + n]
            side = uk[target * CAP + slot]
            here = slice(n * TROWS, (n + 1) * TROWS)
            rows_here = slice((i * TILES + n) * TROWS, (i * TILES + n + 1) * TROWS)
            for j in range(WIDTH // 128):
                cols = slice(j * 128, (j + 1) * 128)
                value = yv[rows_here, cols].astype(F32)
                rg[rows_here, cols] = (inv[here] * (side[:, cols] - value * inn[here])).astype(BF16)

    loads[3].wait()
    lead_y = 1 - lax.div(y, 2)
    lead_z = 1 - lax.div(z, 2)

    def unit(p, first, width):
        part = pl.ds(pl.multiple_of(p * PAIR, PAIR), PAIR)
        cols = slice(first, first + width)
        term = jnp.dot(vt[part, :], rg[:, cols], preferred_element_type=F32)
        carried = term + res[part, cols].astype(F32)
        clipped = jnp.clip(carried, -clip_limit, clip_limit)
        res[part, cols] = (carried - clipped).astype(BF16)
        return clipped[:BLOCK].astype(BF16), clipped[BLOCK:].astype(BF16)

    class Sum:
        def __init__(self, n, q, r, r2, at, near, lead, at2, near2):
            self.n, self.q, self.r, self.r2 = n, q, r, r2
            self.at, self.near, self.lead, self.at2, self.near2 = at, near, lead, at2, near2

        def piece(self, by, i):
            return 2 * step(self.at, by) + lax.rem(self.lead + i, 2)

        def send(self, m, i, by, to):
            recv = q_long.at[self.n, i] if m == 0 else q_near.at[self.n, i]
            start(
                self.q.at[self.piece(by, i)], self.r.at[2 * i + m - 1 if m else 4 + i],
                q_send.at[self.n], recv, self.near(to),
            )

        def long(self, i):
            self.send(0, i, 2, s)

        def long_block(self, i, j):
            start(
                self.q.at[self.piece(2, i), j], self.r.at[4 + i, j],
                q_send.at[self.n], q_long.at[self.n, i], self.near(s),
            )

        def plain(self, i):
            self.send(1, i, -s, -s)

        def middle(self, i):
            done(self.r.at[4 + i], q_long.at[self.n, i])
            self.add(self.piece(s, i), (4 + i,))
            self.send(2, i, s, s)

        def own(self, i):
            done(self.r.at[pl.ds(2 * i, 2)], q_near.at[self.n, i])
            self.add(self.piece(0, i), (2 * i, 2 * i + 1))

        def add(self, index, terms):
            for j in range(2):
                value = self.q[index, j].astype(F32)
                for term in terms:
                    value = value + self.r[term, j].astype(F32)
                self.q[index, j] = value.astype(BF16)

        def block(self, by):
            at2 = step(self.at2, by)
            return (2 * self.at + lax.div(at2, 2), lax.rem(at2, 2))

        def send2(self, m, by, to):
            recv = q2_long.at[self.n] if m == 0 else q2_near.at[self.n]
            start(
                self.q.at[self.block(by)], self.r2.at[(2, 0, 1)[m]],
                q2_send.at[self.n], recv, self.near2(to),
            )

        def long2(self):
            self.send2(0, 2, s)

        def plain2(self):
            self.send2(1, -s, -s)

        def middle2(self):
            done(self.r2.at[2], q2_long.at[self.n])
            here = self.block(s)
            self.q[here] = (self.q[here].astype(F32) + self.r2[2].astype(F32)).astype(BF16)
            self.send2(2, s, s)

        def direct2(self):
            for m in range(1, RING):
                start(
                    self.q.at[self.block(m)], self.r2.at[m - 1],
                    q2_send.at[self.n], q2_near.at[self.n], self.near2(m),
                )

        def finish_direct(self, cols):
            done(self.r2, q2_near.at[self.n])
            total = self.q[self.block(0)].astype(F32)
            for m in range(RING - 1):
                total = total + self.r2[m].astype(F32)
            wg[:, cols] = total

        def finish(self, cols):
            done(self.r2.at[pl.ds(0, 2)], q2_near.at[self.n])
            total = self.q[self.block(0)].astype(F32) + self.r2[0].astype(F32)
            wg[:, cols] = total + self.r2[1].astype(F32)

        def sent(self):
            done(self.r, q_send.at[self.n])
            done(self.r2, q2_send.at[self.n])

    sums = []
    for n, (q_a, r_a, r2_a, q_b, r_b, r2_b) in enumerate(
        ((qa0, ra0, ra20, qb0, rb0, rb20), (qa1, ra1, ra21, qb1, rb1, rb21))
    ):
        sums.append(
            (
                Sum(2 * n, q_a, r_a, r2_a, z, z_dev, lead_y, y, y_dev),
                Sum(2 * n + 1, q_b, r_b, r2_b, y, y_dev, lead_z, z, z_dev),
            )
        )

    def turns(n, begin, end):
        (a, b), (first, width) = sums[n], PARTS[n]

        @pl.loop(begin, end)
        def _(i):
            turn, which = lax.div(i, 2), lax.rem(i, 2)
            by = jnp.where(turn == 0, 2, jnp.where(turn == 1, -s, jnp.where(turn == 2, s, 0)))
            p = 2 * step(z, by) + lax.rem(lead_y + which, 2)
            low, high = unit(p, first, width)
            a.q[p, 0] = low
            a.q[p, 1] = high
            pair = lax.rem(lead_y + lax.div(i, 4), 2)
            plane = lax.rem(2 * lead_z + lax.rem(i, 4), RING)
            for n in range(2):
                pl.when(i == n)(lambda n=n: a.long(n))
                pl.when(i == 2 + n)(lambda n=n: a.plain(n))
            low, high = unit(2 * plane + pair, HALF + first, width)
            b.q[4 * pair + lax.div(plane, 2), lax.rem(plane, 2)] = low
            b.q[4 * pair + 2 + lax.div(plane, 2), lax.rem(plane, 2)] = high
            for n in range(2):
                pl.when(i == 5 + 2 * n)(lambda n=n: b.plain(n))
            for n in range(4):
                pl.when(i == n)(lambda n=n: b.long_block(n // 2, n % 2))

    def middles(n, i):
        for part in sums[n]:
            part.middle(i)

    turns(0, 0, 8)
    turns(1, 0, 4)
    middles(0, 0)
    turns(1, 4, 8)
    middles(0, 1)
    middles(1, 0)
    middles(1, 1)
    early, late = sums
    for i in range(2):
        for part in early:
            part.own(i)
            if i == 0:
                part.long2()
    for part in early:
        part.plain2()
    for i in range(2):
        for part in late:
            part.own(i)
    for part in late:
        part.direct2()
    for part in early:
        part.middle2()
    for pair, (first, width) in zip(sums, PARTS):
        for n, part in enumerate(pair):
            cols = slice(n * HALF + first, n * HALF + first + width)
            part.finish(cols) if pair is early else part.finish_direct(cols)

    done(v.at[pl.ds(0, 7 * ROWS)], v_send.at[0])
    done(k.at[pl.ds(0, 7 * CAP)], k_send.at[0])
    for n in range(CHUNKS):
        done(p_slots(n, 15), p_send.at[n])
    done(st.at[pl.ds(0, GROUPS - 1)], s_send.at[0])
    for pair in sums:
        for part in pair:
            part.sent()


def write_back(grad, left, grad_out, left_out, sems):
    copies = []
    for i in range(WRITES):
        part = pl.ds(i * (ENC // WRITES), ENC // WRITES)
        copies.append(pltpu.make_async_copy(left.at[part], left_out.at[part], sems.at[i]))
    copies.append(pltpu.make_async_copy(grad, grad_out, sems.at[WRITES]))
    for copy in copies:
        copy.start()
    for copy in copies:
        copy.wait()


def per_device(visual, projector, key_weight, norm_gain, cotangent, residual, counts, offsets):
    anywhere = pl.BlockSpec(memory_space=pl.ANY)
    scalars = pl.BlockSpec(memory_space=pltpu.SMEM)
    dma = pltpu.SemaphoreType.DMA
    results = pl.pallas_call(
        kernel,
        out_shape=(
            pltpu.VMEM((BLOCK, WIDTH), F32),
            pltpu.VMEM((ENC, WIDTH), BF16),
        ),
        in_specs=[
            anywhere, anywhere, anywhere, anywhere, anywhere, anywhere, scalars, scalars,
        ],
        out_specs=(pl.BlockSpec(memory_space=pltpu.VMEM),) * 2,
        scratch_shapes=[
            pltpu.VMEM((ALL_ROWS, ENC), BF16),
            pltpu.VMEM((ENC, ALL_ROWS), BF16),
            pltpu.VMEM((2, 16, BLOCK, WIDE), BF16),
            pltpu.VMEM((2, 16, BLOCK, NARROW), BF16),
            pltpu.VMEM((ENC, 2 * WIDE), BF16),
            pltpu.VMEM((ALL_ROWS, WIDTH), BF16),
            pltpu.VMEM((GROUPS * CAP, TROWS, WIDTH), F32),
            pltpu.VMEM((GROUPS * CAP, TROWS, KEYS), BF16),
            pltpu.VMEM((WIDTH, KEYS), BF16),
            pltpu.VMEM((512, KEYS), BF16),
            pltpu.VMEM((SLOT_ROWS, 512), BF16),
            pltpu.VMEM((ALL_ROWS, WIDTH), BF16),
            pltpu.VMEM((WIDTH,), BF16),
            pltpu.VMEM((GROUPS, 2 * GROUPS, 128), F32),
            *[pltpu.VMEM((8, 2, BLOCK, w), BF16) for _, w in PARTS],
            *[pltpu.VMEM((8, 2, BLOCK, w), BF16) for _, w in PARTS],
            *[pltpu.VMEM((6, 2, BLOCK, w), BF16) for _, w in PARTS],
            *[pltpu.VMEM((6, 2, BLOCK, w), BF16) for _, w in PARTS],
            *[pltpu.VMEM((3, BLOCK, w), BF16) for _, w in PARTS],
            *[pltpu.VMEM((3, BLOCK, w), BF16) for _, w in PARTS],
            dma((9,)),
            dma((1,)), dma((3, ROW_PIECES)), dma((4,)),
            dma((1,)), dma((3, KEY_PIECES)), dma((4,)),
            dma((CHUNKS,)), dma((CHUNKS, 7)), dma((CHUNKS,)), dma((1,)), dma((1,)),
            dma((4,)), dma((4, 2)), dma((4, 2)), dma((4,)), dma((4,)), dma((4,)),
        ],
        compiler_params=pltpu.CompilerParams(
            collective_id=0, has_side_effects=True, vmem_limit_bytes=56 * 2**20
        ),
        cost_estimate=pl.CostEstimate(flops=16 * 10**9, bytes_accessed=20 * 10**6, transcendentals=0),
    )(
        visual[0], projector, key_weight, norm_gain, cotangent[0], residual, counts[0], offsets[0]
    )
    grad, left = [pltpu.with_memory_space_constraint(r, pltpu.VMEM) for r in results]
    return pl.pallas_call(
        write_back,
        out_shape=(
            jax.ShapeDtypeStruct((BLOCK, WIDTH), F32),
            jax.ShapeDtypeStruct((ENC, WIDTH), BF16),
        ),
        in_specs=[pl.BlockSpec(memory_space=pltpu.VMEM)] * 2,
        out_specs=(anywhere, anywhere),
        scratch_shapes=[dma((WRITES + 1,))],
        compiler_params=pltpu.CompilerParams(vmem_limit_bytes=2**20),
    )(grad, left)


def solution(mesh):
    placed = (
        P("dp", "grp", None),
        P("dp", "grp"),
        P(),
        P(),
        P("dp", "grp", None),
        P("dp", "grp"),
        P("dp", None, None),
        P("dp", None, None),
    )
    return jax.shard_map(
        per_device,
        mesh=mesh,
        in_specs=placed,
        out_specs=(P("dp", "grp"), P("dp", "grp")),
        check_vma=False,
    )
```
